256 devices in a mesh: row: 32 (over y, z), col: 8 (over x, core).
Axes of the slice: x: 4, y: 4, z: 8, core: 2. Of those that a mesh axis runs over, the one named last changes fastest.
Arguments:
- homolog_embedding: bfloat16 [32, 1024, 256], P('col', 'row'), may hold values from -6 to 6
- standardize_factor: float32 [256], replicated, may hold values from 0.25 to 1.75
- standardize_shift: float32 [256], replicated, may hold values from -3 to 3
- embed_matrices: bfloat16 [256, 64], replicated, may hold values from -0.375 to 0.375
- embed_shifts: float32 [64], replicated, may hold values from -4 to 4
- final_matrix: bfloat16 [1024, 128], replicated, may hold values from -0.1875 to 0.1875
- final_shift: float32 [128], replicated, may hold values from -4 to 4
- contact_update_cotangent: bfloat16 [1024, 1024, 128], P('row', 'col'), may hold values from -6 to 6
Outputs:
- pair_update: bfloat16 [1024, 1024, 128], P('row', 'col')
- alignment_gradient: float32 [32, 1024, 256], P('col', 'row')
- out_weight_grad: float32 [1024, 128], replicated
- proj_weight_grad: float32 [256, 64], replicated
The draws below stay inside these ranges and needn't reach their ends.
All inputs are finite; a program needn't handle non-finite values.
Results may differ from the reference program's by a relative error of at most 0.019.
Values may be sent and summed in bfloat16 or wider, within the bound.
A program may use at most 64 MiB of HBM per device.

```python
import jax
import jax.numpy as jnp
from jax import lax

FEATURE_WIDTH = 256
EMBED_WIDTH = 32
PAIR_CH = 128
HOMOLOG_NUMBER = 32
AMINO_NUMBER = 1024


def block_scale(own_key, shape, pieces, least, largest):
    gain = 1.0
    for axis_at, blocks in pieces:
        steps = jax.random.uniform(jax.random.fold_in(jax.random.fold_in(own_key, 6), axis_at), (blocks,), jnp.float32, least / len(pieces), largest / len(pieces))
        gain = gain * jnp.repeat(jnp.exp(steps), shape[axis_at] // blocks).reshape((-1,) + (1,) * (len(shape) - 1 - axis_at))
    return gain


def noise(own_key, extent, scale, bound, cuts=(), held_as=jnp.bfloat16):
    entries = scale * jax.random.normal(own_key, extent, jnp.float32)
    if cuts:
        entries = entries * block_scale(own_key, extent, cuts, -0.22, 0.18)
    return jnp.clip(entries, -bound, bound).astype(held_as)


def setup_inputs(seed: int = 0) -> dict:
    keys = jax.random.split(jax.random.key(seed), 9)
    homolog_embedding = noise(keys[0], (HOMOLOG_NUMBER, AMINO_NUMBER, FEATURE_WIDTH), 1.0, 6.0, ((0, 8), (1, 32)))
    standardize_factor = jnp.clip(1.0 + 0.15 * jax.random.normal(keys[1], (FEATURE_WIDTH,), jnp.float32), 0.25, 1.75)
    standardize_shift = noise(keys[2], (FEATURE_WIDTH,), 0.5, 3.0, (), jnp.float32)
    embed_matrices = noise(keys[3], (FEATURE_WIDTH, 2 * EMBED_WIDTH), FEATURE_WIDTH ** -0.5, 0.375)
    embed_shifts = noise(keys[4], (2 * EMBED_WIDTH,), 1.0, 4.0, (), jnp.float32)
    final_matrix = noise(keys[5], (EMBED_WIDTH * EMBED_WIDTH, PAIR_CH), (EMBED_WIDTH * EMBED_WIDTH) ** -0.5, 0.1875)
    final_shift = noise(keys[6], (PAIR_CH,), 1.0, 4.0, (), jnp.float32)
    contact_update_cotangent = noise(keys[7], (AMINO_NUMBER, AMINO_NUMBER, PAIR_CH), 1.0, 6.0, ((0, 32), (1, 8)))
    return dict(homolog_embedding=homolog_embedding, standardize_factor=standardize_factor, standardize_shift=standardize_shift, embed_matrices=embed_matrices, embed_shifts=embed_shifts, final_matrix=final_matrix, final_shift=final_shift, contact_update_cotangent=contact_update_cotangent)


def standardized_blocks(homolog_embedding, standardize_factor, standardize_shift):
    tensor_product_entries = homolog_embedding.astype(jnp.float32)
    centre = tensor_product_entries - lax.optimization_barrier(jnp.mean(tensor_product_entries, axis=-1, keepdims=True))
    reciprocal_spread = lax.rsqrt(lax.optimization_barrier(jnp.mean(centre * centre, axis=-1, keepdims=True)) + 1e-05)
    centred_features = centre * reciprocal_spread
    standardized_matrix = (centred_features * standardize_factor + standardize_shift).astype(jnp.bfloat16)
    return (centred_features, reciprocal_spread, standardized_matrix)

def pair_blocks(a_flat, b_flat, final_matrix, final_shift, cotangent, width):
    seqs = a_flat.shape[0]
    rows, cols, pair_ch = cotangent.shape
    step = 8
    inv_seq = 1.0 / seqs

    def one_block(carry, index):
        weight_gradient, dbsum = carry
        a_block = lax.dynamic_slice_in_dim(a_flat, index * (step * width), step * width, 1)
        outer = lax.dot_general(a_block, b_flat, (((0,), (0,)), ((), ())), preferred_element_type=jnp.float32)
        outer = outer.reshape(step, width, cols, width).transpose(0, 2, 1, 3).reshape(step * cols, width * width)
        outer = (outer * inv_seq).astype(jnp.bfloat16)
        grad_rows = lax.dynamic_slice_in_dim(cotangent, index * step, step, 0).reshape(step * cols, pair_ch)
        update = (jnp.dot(outer, final_matrix, preferred_element_type=jnp.float32) + final_shift).astype(jnp.bfloat16)
        douter = lax.dot_general(grad_rows, final_matrix, (((1,), (1,)), ((), ())), preferred_element_type=jnp.float32).astype(jnp.bfloat16)
        weight_gradient = weight_gradient + lax.dot_general(outer, grad_rows, (((0,), (0,)), ((), ())), preferred_element_type=jnp.float32)
        dmixed = douter.reshape(step, cols, width, width).transpose(0, 2, 1, 3).reshape(step * width, cols * width)
        da_block = lax.dot_general(b_flat, dmixed, (((1,), (1,)), ((), ())), preferred_element_type=jnp.float32) * inv_seq
        dbsum = dbsum + jnp.dot(a_block, dmixed, preferred_element_type=jnp.float32)
        return ((weight_gradient, dbsum), (update.reshape(step, cols, pair_ch), da_block))
    start = (jnp.zeros((width * width, pair_ch), jnp.float32), jnp.zeros((seqs, cols * width), jnp.float32))
    indices = jnp.arange(rows // step, dtype=jnp.int32)
    (weight_gradient, dbsum), (updates, da_blocks) = lax.scan(one_block, start, indices)
    pair_state = updates.reshape(rows, cols, pair_ch)
    da_flat = da_blocks.transpose(1, 0, 2).reshape(seqs, rows * width)
    return (pair_state, da_flat, dbsum * inv_seq, weight_gradient)

def norm_gradient_pass(projection_gradient, centred_features, reciprocal_spread, standardized_matrix, standardize_factor, embed_matrices):
    feature_number = standardized_matrix.shape[-1]
    weight_wide = embed_matrices.astype(jnp.float32)
    pair_gradient = jnp.dot(standardized_matrix.astype(jnp.float32).reshape(-1, feature_number).T, projection_gradient.reshape(-1, projection_gradient.shape[-1]), precision=lax.Precision.HIGHEST)
    dnorm = jnp.dot(projection_gradient, weight_wide.T, precision=lax.Precision.HIGHEST) * standardize_factor
    mean_one = lax.optimization_barrier(jnp.mean(dnorm, axis=-1, keepdims=True))
    mean_two = lax.optimization_barrier(jnp.mean(dnorm * centred_features, axis=-1, keepdims=True))
    return (reciprocal_spread * (dnorm - mean_one - centred_features * mean_two), pair_gradient)

def reference(homolog_embedding, standardize_factor, standardize_shift, embed_matrices, embed_shifts, final_matrix, final_shift, contact_update_cotangent):
    centred_features, reciprocal_spread, standardized_matrix = standardized_blocks(homolog_embedding, standardize_factor, standardize_shift)
    proj = (jnp.dot(standardized_matrix, embed_matrices, preferred_element_type=jnp.float32) + embed_shifts).astype(jnp.bfloat16)
    a_flat = proj[..., :EMBED_WIDTH].reshape(HOMOLOG_NUMBER, AMINO_NUMBER * EMBED_WIDTH)
    b_flat = proj[..., EMBED_WIDTH:].reshape(HOMOLOG_NUMBER, AMINO_NUMBER * EMBED_WIDTH)
    pair_state, da_flat, db_flat, weight_gradient = pair_blocks(a_flat, b_flat, final_matrix, final_shift, contact_update_cotangent, EMBED_WIDTH)
    projection_gradient = jnp.concatenate([da_flat.reshape(HOMOLOG_NUMBER, AMINO_NUMBER, EMBED_WIDTH), db_flat.reshape(HOMOLOG_NUMBER, AMINO_NUMBER, EMBED_WIDTH)], axis=-1)
    alignment_gradient, pair_gradient = norm_gradient_pass(projection_gradient, centred_features, reciprocal_spread, standardized_matrix, standardize_factor, embed_matrices)
    return (pair_state, alignment_gradient, weight_gradient * (1.0 / AMINO_NUMBER), pair_gradient * (1.0 / AMINO_NUMBER))
```

```python
import functools

import jax
import jax.numpy as jnp
from jax import lax
from jax.experimental import pallas as pl
from jax.experimental.pallas import tpu as pltpu
from jax.sharding import PartitionSpec as P

BF16 = jnp.bfloat16
F32 = jnp.float32
MESH = pl.DeviceIdType.MESH
LANES = 128


def nt(x, y):
    return lax.dot_general(x, y, (((1,), (1,)), ((), ())), preferred_element_type=F32)


def nn(x, y):
    return lax.dot_general(x, y, (((1,), (0,)), ((), ())), preferred_element_type=F32)


def tn(x, y):
    return lax.dot_general(x, y, (((0,), (0,)), ((), ())), preferred_element_type=F32)


def iota(shape, dim):
    return lax.broadcasted_iota(jnp.int32, shape, dim)


def one_hot(cond):
    return jnp.where(cond, 1.0, 0.0).astype(BF16)


def wait_bytes(ref, sem):
    pltpu.make_async_copy(ref, ref, sem).wait()


def lane_aligned(start):
    return pl.multiple_of(start, LANES)


def kernel(
    rows,
    cols,
    x_ref,
    gain_ref,
    shift_ref,
    we_ref,
    eshift_ref,
    wf_ref,
    fshift_ref,
    g_hbm,
    pair_hbm,
    align_hbm,
    ow_hbm,
    pw_hbm,
    a_all,
    b_all,
    b_piece,
    gmat,
    wf32,
    w4,
    perm,
    gather_rows,
    scatter_rows,
    aw,
    gp,
    pair_buf,
    align_buf,
    ow_buf,
    pw_buf,
    da_out,
    da_in,
    db_out,
    db_in,
    dw_out,
    dw_in,
    dw_mid,
    dw_fin,
    wg_out,
    wg_in,
    wg_mid,
    wg_fin,
    ready,
    out_sem,
    send,
    recv,
):
    sl, block, feat = x_ref.shape
    width = we_ref.shape[1] // 2
    ch = wf_ref.shape[1]
    ratio = rows // cols
    seqs = sl * cols
    j_len = ratio * block
    inv_seq = 1.0 / seqs
    inv_res = 1.0 / (rows * block)
    me_r = lax.axis_index("row")
    me_c = lax.axis_index("col")

    barrier = pltpu.get_barrier_semaphore()

    def greet_row(k, carry):
        pl.semaphore_signal(
            barrier, inc=1, device_id=(lax.rem(me_r + k, rows), me_c), device_id_type=MESH
        )
        return carry

    def greet_col(k, carry):
        pl.semaphore_signal(
            barrier, inc=1, device_id=(me_r, lax.rem(me_c + k, cols)), device_id_type=MESH
        )
        return carry

    lax.fori_loop(1, rows, greet_row, 0)
    lax.fori_loop(1, cols, greet_col, 0)

    for i in range(block):
        pltpu.make_async_copy(
            g_hbm.at[i], gmat.at[:, pl.ds(i * ch, ch)], out_sem.at[0]
        ).start()

    x = x_ref[...].astype(F32).reshape(sl * block, feat)
    centre = x - jnp.mean(x, axis=-1, keepdims=True)
    inv = lax.rsqrt(jnp.mean(centre * centre, axis=-1, keepdims=True) + 1e-05)
    normed = centre * inv
    gain = gain_ref[...]
    lnout = (normed * gain + shift_ref[...]).astype(BF16)
    we = we_ref[...]
    lane2 = iota((2 * width, 2 * LANES), 1)
    tile_map = one_hot(
        iota((2 * width, 2 * LANES), 0) == (lane2 // LANES) * width + lane2 % width
    )
    we4 = nn(we, tile_map).astype(BF16)
    es = eshift_ref[...]
    es4 = jnp.concatenate([es[:, :width]] * sl + [es[:, width:]] * sl, axis=1)
    proj = nn(lnout, we4) + es4
    owner_lane = (iota((block, 2 * LANES), 1) % LANES) // width
    piece = jnp.zeros((block, 2 * LANES), F32)
    for s in range(sl):
        piece = jnp.where(owner_lane == s, proj[s * block : (s + 1) * block], piece)
    piece = piece.astype(BF16)
    a_all[me_c] = piece[:, :LANES]
    b_piece[...] = piece[:, LANES:]

    pl.semaphore_wait(barrier, rows - 1 + cols - 1)

    def confirm(k, carry):
        pl.semaphore_signal(
            ready, inc=1, device_id=(me_r, lax.rem(me_c + k, cols)), device_id_type=MESH
        )
        return carry

    lax.fori_loop(1, cols, confirm, 0)
    pl.semaphore_wait(ready, cols - 1)

    def to_cols(src, dst, phase):
        def body(k, carry):
            peer = lax.rem(me_c + k, cols)
            pltpu.make_async_remote_copy(
                src_ref=src(peer),
                dst_ref=dst,
                send_sem=send.at[phase],
                recv_sem=recv.at[phase],
                device_id=(me_r, peer),
                device_id_type=MESH,
            ).start()
            return carry

        lax.fori_loop(1, cols, body, 0)

    def to_rows(src, dst, phase):
        def body(k, carry):
            peer = lax.rem(me_r + k, rows)
            pltpu.make_async_remote_copy(
                src_ref=src(peer),
                dst_ref=dst,
                send_sem=send.at[phase],
                recv_sem=recv.at[phase],
                device_id=(peer, me_c),
                device_id_type=MESH,
            ).start()
            return carry

        lax.fori_loop(1, rows, body, 0)

    to_cols(lambda peer: a_all.at[me_c], a_all.at[me_c], 0)
    b_col = me_r // ratio
    b_slot = pl.ds(pl.multiple_of((me_r % ratio) * block, block), block)

    def send_b(k, carry):
        peer = lax.rem(me_r + k, rows)
        own = jnp.logical_and(peer == me_r, b_col == me_c)

        @pl.when(jnp.logical_not(own))
        def _():
            pltpu.make_async_remote_copy(
                src_ref=b_piece,
                dst_ref=b_all.at[me_c, b_slot],
                send_sem=send.at[1],
                recv_sem=recv.at[1],
                device_id=(peer, b_col),
                device_id_type=MESH,
            ).start()

        @pl.when(own)
        def _():
            pltpu.make_async_copy(b_piece, b_all.at[me_c, b_slot], recv.at[1]).start()

        return carry

    lax.fori_loop(0, rows, send_b, 0)

    wf32[...] = wf_ref[...].astype(F32)
    for e in range(width):
        block_e = wf32[pl.ds(e, width, stride=width), :].astype(BF16)
        for s in range(sl):
            w4[s * width : (s + 1) * width, e * ch : (e + 1) * ch] = block_e

    es_len = seqs * width
    step = min(256, es_len)
    for r0 in range(0, es_len, step):
        at_row = iota((step, es_len), 0) + r0
        at_lane = iota((step, es_len), 1)
        perm[r0 : r0 + step, :] = one_hot(
            at_lane == (at_row % seqs) * width + at_row // seqs
        )
    is_len = block * seqs
    qi_len = block * cols
    at_row = iota((is_len, qi_len), 0)
    gather_rows[...] = one_hot(
        iota((is_len, qi_len), 1) == ((at_row % seqs) // sl) * block + at_row // seqs
    )
    at_lane = iota((qi_len, is_len), 1)
    scatter_rows[...] = one_hot(
        iota((qi_len, is_len), 0) == ((at_lane % seqs) // sl) * block + at_lane // seqs
    )
    own_seq = iota((is_len, LANES), 0) % sl == iota((is_len, LANES), 1) // width

    wait_bytes(a_all.at[pl.ds(0, cols - 1)], recv.at[0])
    a_cat = a_all[...].reshape(qi_len, LANES)
    a_rows = (jnp.where(own_seq, nn(gather_rows[...], a_cat), 0.0) * inv_seq).astype(BF16)
    pair_lanes = 2 * ch

    def make_aw(n, carry):
        res = nn(a_rows, w4[:, pl.ds(lane_aligned(n * pair_lanes), pair_lanes)]).astype(BF16)
        for el in range(2):
            at = pl.ds(pl.multiple_of((2 * n + el) * seqs, seqs), seqs)
            for i in range(block):
                aw[at, i * ch : (i + 1) * ch] = res[
                    i * seqs : (i + 1) * seqs, el * ch : (el + 1) * ch
                ]
        return carry

    lax.fori_loop(0, width // 2, make_aw, 0)

    wait_bytes(gmat, out_sem.at[0])
    db_es = jnp.concatenate(
        [nt(gmat[...], aw[n : n + step, :]).astype(BF16) for n in range(0, es_len, step)],
        axis=1,
    )
    db_se = nn(db_es, perm[...]).astype(BF16)
    for q in range(cols):
        db_out[q] = db_se[:, q * LANES : (q + 1) * LANES]

    def send_db(t, carry):
        idx = lax.rem(t + me_r, rows)
        row_to = ratio * me_c + idx // cols
        col_to = idx % cols
        src = db_out.at[col_to, pl.ds(pl.multiple_of((idx // cols) * block, block), block)]
        own = jnp.logical_and(row_to == me_r, col_to == me_c)

        @pl.when(jnp.logical_not(own))
        def _():
            pltpu.make_async_remote_copy(
                src_ref=src,
                dst_ref=db_in.at[me_r],
                send_sem=send.at[3],
                recv_sem=recv.at[3],
                device_id=(row_to, col_to),
                device_id_type=MESH,
            ).start()

        @pl.when(own)
        def _():
            pltpu.make_async_copy(src, db_in.at[me_r], recv.at[3]).start()

        return carry

    lax.fori_loop(0, rows, send_db, 0)

    wait_bytes(b_all, recv.at[1])
    b_cat = jnp.concatenate([b_all[q] for q in range(cols)], axis=1)
    b_t = nt(perm[...], b_cat).astype(BF16)
    b_es = nt(b_cat, perm[...]).astype(BF16)

    def make_g(n, carry):
        res = nn(b_t, gmat[:, pl.ds(lane_aligned(n * pair_lanes), pair_lanes)]).astype(BF16)
        for il in range(2):
            at = pl.ds(pl.multiple_of((2 * n + il) * seqs, seqs), seqs)
            for e in range(width):
                gp[at, e * ch : (e + 1) * ch] = res[
                    e * seqs : (e + 1) * seqs, il * ch : (il + 1) * ch
                ]
        return carry

    lax.fori_loop(0, block // 2, make_g, 0)

    step = min(256, is_len)
    da_rows = jnp.concatenate(
        [nt(gp[n : n + step, :], w4[...]) * inv_seq for n in range(0, is_len, step)], axis=0
    )
    da_rows = jnp.where(own_seq, da_rows, 0.0).astype(BF16)
    da_out[...] = nn(scatter_rows[...], da_rows).astype(BF16).reshape(cols, block, LANES)
    to_cols(lambda peer: da_out.at[peer], da_in.at[me_c], 2)
    da_in[me_c] = da_out[me_c]

    folded = functools.reduce(
        lambda u, v: u + v,
        [a_rows.astype(F32).T[s * width : (s + 1) * width] for s in range(sl)],
    ).astype(BF16)

    def make_dw(n, carry):
        res = nn(folded, gp[:, pl.ds(lane_aligned(n * pair_lanes), pair_lanes)]).astype(BF16)
        for el in range(2):
            dw_out[2 * n + el] = res[:, el * ch : (el + 1) * ch]
        return carry

    lax.fori_loop(0, width // 2, make_dw, 0)
    per_row = width // rows
    to_rows(lambda peer: dw_out.at[pl.ds(peer * per_row, per_row)], dw_in.at[me_r], 4)
    dw_in[me_r] = dw_out[pl.ds(me_r * per_row, per_row)]

    fshift = fshift_ref[...]

    def make_pair(n, carry):
        res = nn(b_es, aw[:, pl.ds(lane_aligned(n * pair_lanes), pair_lanes)])
        for il in range(2):
            pair_buf[2 * n + il] = (res[:, il * ch : (il + 1) * ch] + fshift).astype(BF16)
        at = pl.ds(2 * n, 2)
        pltpu.make_async_copy(pair_buf.at[at], pair_hbm.at[at], out_sem.at[1]).start()
        return carry

    lax.fori_loop(0, block // 2, make_pair, 0)

    wait_bytes(da_in.at[pl.ds(0, cols - 1)], recv.at[2])
    wait_bytes(db_in, recv.at[3])
    da = jnp.sum(da_in[...].astype(F32), axis=0)
    db = jnp.sum(db_in[...].astype(F32), axis=0)
    dproj = jnp.concatenate([da, db], axis=1)
    dproj = jnp.concatenate(
        [jnp.where(owner_lane == s, dproj, 0.0) for s in range(sl)], axis=0
    )
    high = dproj.astype(BF16)
    low = (dproj - high.astype(F32)).astype(BF16)
    wg = tn(high, lnout) + tn(low, lnout)
    wg = jnp.concatenate(
        [
            functools.reduce(
                lambda u, v: u + v,
                [wg[h + s * width : h + (s + 1) * width] for s in range(sl)],
            )
            for h in (0, LANES)
        ],
        axis=0,
    )
    halves = feat // LANES
    part = halves * 2 * width // cols
    wg = jnp.concatenate([wg[:, h * LANES : (h + 1) * LANES] for h in range(halves)], axis=0)
    wg_out[...] = wg.astype(BF16).reshape(cols, part, LANES)
    to_cols(lambda peer: wg_out.at[peer], wg_in.at[me_c], 7)
    wg_in[me_c] = wg_out[me_c]

    wait_bytes(dw_in.at[pl.ds(0, rows - 1)], recv.at[4])
    dw_mid[me_c] = jnp.sum(dw_in[...].astype(F32), axis=0).astype(BF16)
    to_cols(lambda peer: dw_mid.at[me_c], dw_mid.at[me_c], 5)

    dnorm = (nt(high, we4) + nt(low, we4)) * gain
    mean_one = jnp.mean(dnorm, axis=-1, keepdims=True)
    mean_two = jnp.mean(dnorm * normed, axis=-1, keepdims=True)
    align_buf[...] = (inv * (dnorm - mean_one - normed * mean_two)).reshape(sl, block, feat)
    align_copy = pltpu.make_async_copy(align_buf, align_hbm, out_sem.at[2])
    align_copy.start()

    wait_bytes(wg_in.at[pl.ds(0, cols - 1)], recv.at[7])
    wg_mid[me_r] = jnp.sum(wg_in[...].astype(F32), axis=0).astype(BF16)
    to_rows(lambda peer: wg_mid.at[me_r], wg_mid.at[me_r], 8)

    wait_bytes(dw_mid.at[pl.ds(0, cols - 1)], recv.at[5])
    dw_fin[me_r] = (jnp.sum(dw_mid[...].astype(F32), axis=0) * inv_res).astype(BF16)
    to_rows(lambda peer: dw_fin.at[me_r], dw_fin.at[me_r], 6)

    wait_bytes(wg_mid.at[pl.ds(0, rows - 1)], recv.at[8])
    wg_fin[me_c] = (jnp.sum(wg_mid[...].astype(F32), axis=0) * inv_res).astype(BF16)
    to_cols(lambda peer: wg_fin.at[me_c], wg_fin.at[me_c], 9)

    wait_bytes(dw_fin.at[pl.ds(0, rows - 1)], recv.at[6])
    for r in range(rows):
        for k in range(per_row):
            ow_buf[pl.ds(r * per_row + k, width, stride=width), :] = dw_fin[r, k].astype(F32)
    ow_copy = pltpu.make_async_copy(ow_buf, ow_hbm, out_sem.at[3])
    ow_copy.start()

    wait_bytes(wg_fin.at[pl.ds(0, cols - 1)], recv.at[9])
    fin = wg_fin[...].reshape(halves * 2 * width, LANES).astype(F32)
    for h in range(halves):
        pw_buf[h * LANES : (h + 1) * LANES, :] = fin[h * 2 * width : (h + 1) * 2 * width].T
    pw_copy = pltpu.make_async_copy(pw_buf, pw_hbm, out_sem.at[4])
    pw_copy.start()

    wait_bytes(a_all.at[pl.ds(0, cols - 1)], send.at[0])
    for phase in (1, 3):

        @pl.when(b_col == me_c)
        def _():
            wait_bytes(db_in.at[pl.ds(0, rows - 1)], send.at[phase])

        @pl.when(b_col != me_c)
        def _():
            wait_bytes(db_in, send.at[phase])

    wait_bytes(da_in.at[pl.ds(0, cols - 1)], send.at[2])
    wait_bytes(dw_in.at[pl.ds(0, rows - 1)], send.at[4])
    wait_bytes(dw_mid.at[pl.ds(0, cols - 1)], send.at[5])
    wait_bytes(dw_fin.at[pl.ds(0, rows - 1)], send.at[6])
    wait_bytes(wg_in.at[pl.ds(0, cols - 1)], send.at[7])
    wait_bytes(wg_mid.at[pl.ds(0, rows - 1)], send.at[8])
    wait_bytes(wg_fin.at[pl.ds(0, cols - 1)], send.at[9])
    wait_bytes(pair_buf, out_sem.at[1])
    align_copy.wait()
    ow_copy.wait()
    pw_copy.wait()


def on_device(x, gain, shift, we, eshift, wf, fshift, g):
    rows = lax.axis_size("row")
    cols = lax.axis_size("col")
    sl, block, feat = x.shape
    width = we.shape[1] // 2
    ch = wf.shape[1]
    j_len = g.shape[1]
    seqs = sl * cols
    per_row = width // rows
    part = feat * 2 * width // LANES // cols
    vmem = pl.BlockSpec(memory_space=pltpu.VMEM)
    hbm = pl.BlockSpec(memory_space=pl.ANY)

    def buf(*shape, dtype=BF16):
        return pltpu.VMEM(shape, dtype)

    return pl.pallas_call(
        functools.partial(kernel, rows, cols),
        out_shape=[
            jax.ShapeDtypeStruct((block, j_len, ch), BF16),
            jax.ShapeDtypeStruct((sl, block, feat), F32),
            jax.ShapeDtypeStruct((width * width, ch), F32),
            jax.ShapeDtypeStruct((feat, 2 * width), F32),
        ],
        in_specs=[vmem] * 7 + [hbm],
        out_specs=[hbm] * 4,
        scratch_shapes=[
            buf(cols, block, LANES),
            buf(cols, j_len, LANES),
            buf(block, LANES),
            buf(j_len, block * ch),
            buf(width * width, ch, dtype=F32),
            buf(LANES, width * ch),
            buf(seqs * width, seqs * width),
            buf(block * seqs, cols * block),
            buf(cols * block, block * seqs),
            buf(width * seqs, block * ch),
            buf(block * seqs, width * ch),
            buf(block, j_len, ch),
            buf(sl, block, feat, dtype=F32),
            buf(width * width, ch, dtype=F32),
            buf(feat, 2 * width, dtype=F32),
            buf(cols, block, LANES),
            buf(cols, block, LANES),
            buf(cols, j_len, LANES),
            buf(rows, block, LANES),
            buf(width, width, ch),
            buf(rows, per_row, width, ch),
            buf(cols, per_row, width, ch),
            buf(rows, per_row, width, ch),
            buf(cols, part, LANES),
            buf(cols, part, LANES),
            buf(rows, part, LANES),
            buf(cols, part, LANES),
            pltpu.SemaphoreType.REGULAR,
            pltpu.SemaphoreType.DMA((5,)),
            pltpu.SemaphoreType.DMA((10,)),
            pltpu.SemaphoreType.DMA((10,)),
        ],
        compiler_params=pltpu.CompilerParams(
            collective_id=0, has_side_effects=True, vmem_limit_bytes=56 * 1024 * 1024
        ),
        cost_estimate=pl.CostEstimate(
            flops=5_000_000_000, bytes_accessed=4_000_000, transcendentals=0
        ),
    )(
        x,
        gain.reshape(1, -1),
        shift.reshape(1, -1),
        we,
        eshift.reshape(1, -1),
        wf,
        fshift.reshape(1, -1),
        g,
    )


def solution(mesh):
    in_specs = (P("col", "row", None), P(), P(), P(), P(), P(), P(), P("row", "col", None))
    out_specs = (P("row", "col", None), P("col", "row", None), P(), P())
    return jax.shard_map(
        on_device, mesh=mesh, in_specs=in_specs, out_specs=out_specs, check_vma=False
    )
```

```python
import functools

import jax
import jax.numpy as jnp
from jax import lax
from jax.experimental import pallas as pl
from jax.experimental.pallas import tpu as pltpu
from jax.sharding import PartitionSpec as P

BF16 = jnp.bfloat16
F32 = jnp.float32
MESH = pl.DeviceIdType.MESH
LANES = 128


def nt(x, y):
    return lax.dot_general(x, y, (((1,), (1,)), ((), ())), preferred_element_type=F32)


def nn(x, y):
    return lax.dot_general(x, y, (((1,), (0,)), ((), ())), preferred_element_type=F32)


def tn(x, y):
    return lax.dot_general(x, y, (((0,), (0,)), ((), ())), preferred_element_type=F32)


def iota(shape, dim):
    return lax.broadcasted_iota(jnp.int32, shape, dim)


def one_hot(cond):
    return jnp.where(cond, 1.0, 0.0).astype(BF16)


def wait_bytes(ref, sem):
    pltpu.make_async_copy(ref, ref, sem).wait()


def lane_aligned(start):
    return pl.multiple_of(start, LANES)


def kernel(
    rows,
    cols,
    x_hbm,
    we_hbm,
    gain_hbm,
    shift_hbm,
    eshift_hbm,
    fshift_hbm,
    wf_hbm,
    g_hbm,
    pair_hbm,
    align_hbm,
    ow_hbm,
    pw_hbm,
    x_ref,
    we_ref,
    gain_ref,
    shift_ref,
    eshift_ref,
    fshift_ref,
    wf_ref,
    a_all,
    b_all,
    b_piece,
    b_relay,
    gmat,
    wf32,
    w4,
    perm,
    gather_rows,
    scatter_rows,
    aw,
    gp,
    pair_buf,
    align_buf,
    ow_buf,
    pw_buf,
    da_out,
    da_in,
    db_out,
    db_in,
    dw_out,
    dw_in,
    dw_mid,
    dw_fin,
    wg_out,
    wg_in,
    wg_mid,
    wg_fin,
    ready,
    in_sem,
    out_sem,
    send,
    recv,
):
    sl, block, feat = x_ref.shape
    width = we_ref.shape[0] // 2
    ch = wf_ref.shape[1]
    ratio = rows // cols
    seqs = sl * cols
    j_len = ratio * block
    inv_seq = 1.0 / seqs
    inv_res = 1.0 / (rows * block)
    me_r = lax.axis_index("row")
    me_c = lax.axis_index("col")
    near = cols // 2
    nz = rows // near
    y, z = me_r // nz, lax.rem(me_r, nz)
    x, core = me_c // 2, lax.rem(me_c, 2)
    group = near * cols
    member = y * cols + me_c

    def in_group(m):
        return ((m // cols) * nz + z, lax.rem(m, cols))

    def in_z(k):
        return (y * nz + k, me_c)

    barrier = pltpu.get_barrier_semaphore()

    def greet_group(k, carry):
        pl.semaphore_signal(
            barrier,
            inc=1,
            device_id=in_group(lax.rem(member + k, group)),
            device_id_type=MESH,
        )
        return carry

    def greet_z(k, carry):
        pl.semaphore_signal(
            barrier, inc=1, device_id=in_z(lax.rem(z + k, nz)), device_id_type=MESH
        )
        return carry

    loads = [
        pltpu.make_async_copy(src, dst, in_sem.at[k])
        for k, (src, dst) in enumerate(
            (
                (x_hbm, x_ref),
                (we_hbm, we_ref),
                (gain_hbm, gain_ref),
                (shift_hbm, shift_ref),
                (eshift_hbm, eshift_ref),
                (fshift_hbm, fshift_ref),
                (wf_hbm, wf_ref),
            )
        )
    ]
    for load in loads:
        load.start()
    lax.fori_loop(1, group, greet_group, 0)
    lax.fori_loop(1, nz, greet_z, 0)

    for i in range(block):
        pltpu.make_async_copy(
            g_hbm.at[i], gmat.at[:, pl.ds(i * ch, ch)], out_sem.at[0]
        ).start()

    loads[0].wait()
    xf = x_ref[...].astype(F32).reshape(sl * block, feat)
    centre = xf - jnp.mean(xf, axis=-1, keepdims=True)
    inv = lax.rsqrt(jnp.mean(centre * centre, axis=-1, keepdims=True) + 1e-05)
    normed = centre * inv
    for load in loads[1:-1]:
        load.wait()
    gain = gain_ref[...]
    lnout = (normed * gain + shift_ref[...]).astype(BF16)
    we = we_ref[...]
    we4 = jnp.concatenate([we[:width]] * sl + [we[width:]] * sl, axis=0)
    es = eshift_ref[...]
    es4 = jnp.concatenate([es[:, :width]] * sl + [es[:, width:]] * sl, axis=1)
    fshift = fshift_ref[...]
    proj = nt(lnout, we4) + es4
    owner_lane = (iota((block, 2 * LANES), 1) % LANES) // width
    piece = jnp.zeros((block, 2 * LANES), F32)
    for s in range(sl):
        piece = jnp.where(owner_lane == s, proj[s * block : (s + 1) * block], piece)
    piece = piece.astype(BF16)
    a_all[me_c] = piece[:, :LANES]
    b_piece[...] = piece[:, LANES:]

    pl.semaphore_wait(barrier, group - 1 + nz - 1)

    def send_all(count, peer_of, device_of, src, dst, phase):
        def body(k, carry):
            peer = peer_of(k)
            pltpu.make_async_remote_copy(
                src_ref=src(peer),
                dst_ref=dst,
                send_sem=send.at[phase],
                recv_sem=recv.at[phase],
                device_id=device_of(peer),
                device_id_type=MESH,
            ).start()
            return carry

        lax.fori_loop(1, count, body, 0)

    def to_cols(src, dst, phase):
        send_all(
            cols, lambda k: lax.rem(me_c + k, cols), lambda p: (me_r, p), src, dst, phase
        )

    def to_group(src, dst, phase):
        send_all(group, lambda k: lax.rem(member + k, group), in_group, src, dst, phase)

    def to_z(src, dst, phase):
        send_all(nz, lambda k: lax.rem(z + k, nz), in_z, src, dst, phase)

    to_cols(lambda peer: a_all.at[me_c], a_all.at[me_c], 0)
    relay = pltpu.make_async_remote_copy(
        src_ref=b_piece,
        dst_ref=b_relay,
        send_sem=send.at[1],
        recv_sem=recv.at[1],
        device_id=(x * nz + z, y * 2 + core),
        device_id_type=MESH,
    )

    @pl.when(x != y)
    def _():
        relay.start()

    @pl.when(x == y)
    def _():
        pltpu.make_async_copy(b_piece, b_relay, recv.at[1]).start()

    def confirm(k, carry):
        pl.semaphore_signal(
            ready,
            inc=1,
            device_id=in_group(lax.rem(member + k, group)),
            device_id_type=MESH,
        )
        return carry

    lax.fori_loop(1, group, confirm, 0)

    loads[-1].wait()
    wf32[...] = wf_ref[...].astype(F32)
    for e in range(width):
        block_e = wf32[pl.ds(e, width, stride=width), :].astype(BF16)
        for s in range(sl):
            w4[s * width : (s + 1) * width, e * ch : (e + 1) * ch] = block_e

    es_len = seqs * width
    step = min(256, es_len)
    for r0 in range(0, es_len, step):
        at_row = iota((step, es_len), 0) + r0
        at_lane = iota((step, es_len), 1)
        perm[r0 : r0 + step, :] = one_hot(
            at_lane == (at_row % seqs) * width + at_row // seqs
        )
    is_len = block * seqs
    qi_len = block * cols
    at_row = iota((is_len, qi_len), 0)
    gather_rows[...] = one_hot(
        iota((is_len, qi_len), 1) == ((at_row % seqs) // sl) * block + at_row // seqs
    )
    at_lane = iota((qi_len, is_len), 1)
    scatter_rows[...] = one_hot(
        iota((qi_len, is_len), 0) == ((at_lane % seqs) // sl) * block + at_lane // seqs
    )
    own_seq = iota((is_len, LANES), 0) % sl == iota((is_len, LANES), 1) // width

    pl.semaphore_wait(ready, group - 1)
    wait_bytes(b_relay, recv.at[1])
    b_col = x * 2 + z // ratio
    b_slot = pl.ds(pl.multiple_of(lax.rem(z, ratio) * block, block), block)
    b_from = y * 2 + core

    def send_b(k, carry):
        peer = lax.rem(me_r + k, rows)
        own = jnp.logical_and(peer == me_r, b_col == me_c)

        @pl.when(jnp.logical_not(own))
        def _():
            pltpu.make_async_remote_copy(
                src_ref=b_relay,
                dst_ref=b_all.at[b_from, b_slot],
                send_sem=send.at[2],
                recv_sem=recv.at[2],
                device_id=(peer, b_col),
                device_id_type=MESH,
            ).start()

        @pl.when(own)
        def _():
            pltpu.make_async_copy(b_relay, b_all.at[b_from, b_slot], recv.at[2]).start()

        return carry

    lax.fori_loop(0, rows, send_b, 0)

    wait_bytes(a_all.at[pl.ds(0, cols - 1)], recv.at[0])
    a_cat = a_all[...].reshape(qi_len, LANES)
    a_rows = (jnp.where(own_seq, nn(gather_rows[...], a_cat), 0.0) * inv_seq).astype(BF16)
    pair_lanes = 2 * ch

    def make_aw(n, carry):
        res = nn(a_rows, w4[:, pl.ds(lane_aligned(n * pair_lanes), pair_lanes)]).astype(BF16)
        for el in range(2):
            at = pl.ds(pl.multiple_of((2 * n + el) * seqs, seqs), seqs)
            for i in range(block):
                aw[at, i * ch : (i + 1) * ch] = res[
                    i * seqs : (i + 1) * seqs, el * ch : (el + 1) * ch
                ]
        return carry

    lax.fori_loop(0, width // 2, make_aw, 0)

    wait_bytes(gmat, out_sem.at[0])
    db_es = jnp.concatenate(
        [nt(gmat[...], aw[n : n + step, :]).astype(BF16) for n in range(0, es_len, step)],
        axis=1,
    )
    db_se = nn(db_es, perm[...]).astype(BF16)
    for q in range(cols):
        db_out[q] = db_se[:, q * LANES : (q + 1) * LANES]

    def send_db(t, carry):
        idx = lax.rem(t + me_r, rows)
        row_to = ratio * me_c + idx // cols
        col_to = idx % cols
        src = db_out.at[col_to, pl.ds(pl.multiple_of((idx // cols) * block, block), block)]
        own = jnp.logical_and(row_to == me_r, col_to == me_c)

        @pl.when(jnp.logical_not(own))
        def _():
            pltpu.make_async_remote_copy(
                src_ref=src,
                dst_ref=db_in.at[me_r],
                send_sem=send.at[3],
                recv_sem=recv.at[3],
                device_id=(row_to, col_to),
                device_id_type=MESH,
            ).start()

        @pl.when(own)
        def _():
            pltpu.make_async_copy(src, db_in.at[me_r], recv.at[3]).start()

        return carry

    lax.fori_loop(0, rows, send_db, 0)

    wait_bytes(b_all, recv.at[2])
    b_cat = jnp.concatenate([b_all[q] for q in range(cols)], axis=1)
    b_t = nt(perm[...], b_cat).astype(BF16)
    b_es = nt(b_cat, perm[...]).astype(BF16)

    def make_g(n, carry):
        res = nn(b_t, gmat[:, pl.ds(lane_aligned(n * pair_lanes), pair_lanes)]).astype(BF16)
        for il in range(2):
            at = pl.ds(pl.multiple_of((2 * n + il) * seqs, seqs), seqs)
            for e in range(width):
                gp[at, e * ch : (e + 1) * ch] = res[
                    e * seqs : (e + 1) * seqs, il * ch : (il + 1) * ch
                ]
        return carry

    lax.fori_loop(0, block // 2, make_g, 0)

    folded = functools.reduce(
        lambda u, v: u + v,
        [a_rows.astype(F32).T[s * width : (s + 1) * width] for s in range(sl)],
    ).astype(BF16)

    def make_dw(n, carry):
        res = nn(folded, gp[:, pl.ds(lane_aligned(n * pair_lanes), pair_lanes)]).astype(BF16)
        for el in range(2):
            dw_out[2 * n + el] = res[:, el * ch : (el + 1) * ch]
        return carry

    lax.fori_loop(0, width // 2, make_dw, 0)
    share = width // group
    to_group(lambda peer: dw_out.at[pl.ds(peer * share, share)], dw_in.at[member], 5)
    dw_in[member] = dw_out[pl.ds(member * share, share)]

    step = min(256, is_len)
    da_rows = jnp.concatenate(
        [nt(gp[n : n + step, :], w4[...]) * inv_seq for n in range(0, is_len, step)], axis=0
    )
    da_rows = jnp.where(own_seq, da_rows, 0.0).astype(BF16)
    da_out[...] = nn(scatter_rows[...], da_rows).astype(BF16).reshape(cols, block, LANES)
    to_cols(lambda peer: da_out.at[peer], da_in.at[me_c], 4)
    da_in[me_c] = da_out[me_c]

    def make_pair(n, carry):
        res = nn(b_es, aw[:, pl.ds(lane_aligned(n * pair_lanes), pair_lanes)])
        for il in range(2):
            pair_buf[2 * n + il] = (res[:, il * ch : (il + 1) * ch] + fshift).astype(BF16)
        at = pl.ds(2 * n, 2)
        pltpu.make_async_copy(pair_buf.at[at], pair_hbm.at[at], out_sem.at[1]).start()
        return carry

    lax.fori_loop(0, block // 4, make_pair, 0)

    wait_bytes(da_in.at[pl.ds(0, cols - 1)], recv.at[4])
    wait_bytes(db_in, recv.at[3])
    da = jnp.sum(da_in[...].astype(F32), axis=0)
    db = jnp.sum(db_in[...].astype(F32), axis=0)
    dproj = jnp.concatenate([da, db], axis=1)
    dproj = jnp.concatenate(
        [jnp.where(owner_lane == s, dproj, 0.0) for s in range(sl)], axis=0
    )
    high = dproj.astype(BF16)
    low = (dproj - high.astype(F32)).astype(BF16)
    wg = tn(high, lnout) + tn(low, lnout)
    wg = jnp.concatenate(
        [
            functools.reduce(
                lambda u, v: u + v,
                [wg[h + s * width : h + (s + 1) * width] for s in range(sl)],
            )
            for h in (0, LANES)
        ],
        axis=0,
    )
    halves = feat // LANES
    part = halves * 2 * width // group
    for h in range(halves):
        for k in range(2 * width // part):
            wg_out[h * 2 * width // part + k] = wg[
                k * part : (k + 1) * part, h * LANES : (h + 1) * LANES
            ]
    to_group(lambda peer: wg_out.at[peer], wg_in.at[member], 8)
    wg_in[member] = wg_out[member]

    lax.fori_loop(block // 4, block // 2, make_pair, 0)

    wait_bytes(dw_in.at[pl.ds(0, group - 1)], recv.at[5])
    dw_mid[z] = jnp.sum(dw_in[...].astype(F32), axis=0).astype(BF16)
    to_z(lambda peer: dw_mid.at[z], dw_mid.at[z], 6)

    dnorm = (nn(high, we4) + nn(low, we4)) * gain
    mean_one = jnp.mean(dnorm, axis=-1, keepdims=True)
    mean_two = jnp.mean(dnorm * normed, axis=-1, keepdims=True)
    align_buf[...] = (inv * (dnorm - mean_one - normed * mean_two)).reshape(sl, block, feat)
    align_copy = pltpu.make_async_copy(align_buf, align_hbm, out_sem.at[2])
    align_copy.start()

    wait_bytes(wg_in.at[pl.ds(0, group - 1)], recv.at[8])
    wg_mid[z] = jnp.sum(wg_in[...], axis=0)
    to_z(lambda peer: wg_mid.at[z], wg_mid.at[z], 9)

    wait_bytes(dw_mid.at[pl.ds(0, nz - 1)], recv.at[6])
    dw_fin[member] = (jnp.sum(dw_mid[...].astype(F32), axis=0) * inv_res).astype(BF16)
    to_group(lambda peer: dw_fin.at[member], dw_fin.at[member], 7)

    wait_bytes(wg_mid.at[pl.ds(0, nz - 1)], recv.at[9])
    wg_fin[member] = jnp.sum(wg_mid[...], axis=0) * inv_res
    to_group(lambda peer: wg_fin.at[member], wg_fin.at[member], 10)

    wait_bytes(dw_fin.at[pl.ds(0, group - 1)], recv.at[7])
    for m in range(group):
        for k in range(share):
            ow_buf[pl.ds(m * share + k, width, stride=width), :] = dw_fin[m, k].astype(F32)
    ow_copy = pltpu.make_async_copy(ow_buf, ow_hbm, out_sem.at[3])
    ow_copy.start()

    wait_bytes(wg_fin.at[pl.ds(0, group - 1)], recv.at[10])
    for h in range(halves):
        for k in range(2 * width // part):
            pw_buf[k * part : (k + 1) * part, h * LANES : (h + 1) * LANES] = wg_fin[
                h * 2 * width // part + k
            ]
    pw_copy = pltpu.make_async_copy(pw_buf, pw_hbm, out_sem.at[4])
    pw_copy.start()

    wait_bytes(a_all.at[pl.ds(0, cols - 1)], send.at[0])

    @pl.when(x != y)
    def _():
        relay.wait_send()

    @pl.when(b_col == me_c)
    def _():
        wait_bytes(db_in.at[pl.ds(0, rows - 1)], send.at[2])

    @pl.when(b_col != me_c)
    def _():
        wait_bytes(db_in, send.at[2])

    @pl.when(me_r // ratio == me_c)
    def _():
        wait_bytes(db_in.at[pl.ds(0, rows - 1)], send.at[3])

    @pl.when(me_r // ratio != me_c)
    def _():
        wait_bytes(db_in, send.at[3])

    wait_bytes(da_in.at[pl.ds(0, cols - 1)], send.at[4])
    wait_bytes(dw_in.at[pl.ds(0, group - 1)], send.at[5])
    wait_bytes(dw_mid.at[pl.ds(0, nz - 1)], send.at[6])
    wait_bytes(dw_fin.at[pl.ds(0, group - 1)], send.at[7])
    wait_bytes(wg_in.at[pl.ds(0, group - 1)], send.at[8])
    wait_bytes(wg_mid.at[pl.ds(0, nz - 1)], send.at[9])
    wait_bytes(wg_fin.at[pl.ds(0, group - 1)], send.at[10])
    wait_bytes(pair_buf, out_sem.at[1])
    align_copy.wait()
    ow_copy.wait()
    pw_copy.wait()


def copy_kernel(*refs):
    sem = refs[-1]
    parts = []
    for src, held, dst in zip(refs[0:4], refs[8:12], refs[4:8]):
        count = 4 if src.shape[0] * src.shape[1] >= 1024 else 1
        rows = src.shape[0] // count
        for k in range(count):
            at = pl.ds(k * rows, rows)
            n = len(parts)
            parts.append(
                (
                    pltpu.make_async_copy(src.at[at], held.at[at], sem.at[0, n]),
                    pltpu.make_async_copy(held.at[at], dst.at[at], sem.at[1, n]),
                )
            )
    for load, _ in parts:
        load.start()
    for load, store in parts:
        load.wait()
        store.start()
    for _, store in parts:
        store.wait()


def on_device(x, gain, shift, we, eshift, wf, fshift, g):
    rows = lax.axis_size("row")
    cols = lax.axis_size("col")
    sl, block, feat = x.shape
    width = we.shape[1] // 2
    ch = wf.shape[1]
    j_len = g.shape[1]
    seqs = sl * cols
    near = cols // 2
    nz = rows // near
    group = near * cols
    share = width // group
    part = feat * 2 * width // LANES // group
    hbm = pl.BlockSpec(memory_space=pl.ANY)

    def buf(*shape, dtype=BF16):
        return pltpu.VMEM(shape, dtype)

    shapes = [
        jax.ShapeDtypeStruct((block, j_len, ch), BF16),
        jax.ShapeDtypeStruct((sl, block, feat), F32),
        jax.ShapeDtypeStruct((width * width, ch), F32),
        jax.ShapeDtypeStruct((2 * width, feat), F32),
    ]
    outs = pl.pallas_call(
        functools.partial(kernel, rows, cols),
        out_shape=shapes,
        in_specs=[hbm] * 8,
        out_specs=[hbm] * 4,
        scratch_shapes=[
            buf(sl, block, feat),
            buf(2 * width, feat),
            buf(1, feat, dtype=F32),
            buf(1, feat, dtype=F32),
            buf(1, 2 * width, dtype=F32),
            buf(1, ch, dtype=F32),
            buf(width * width, ch),
            buf(cols, block, LANES),
            buf(cols, j_len, LANES),
            buf(block, LANES),
            buf(block, LANES),
            buf(j_len, block * ch),
            buf(width * width, ch, dtype=F32),
            buf(LANES, width * ch),
            buf(seqs * width, seqs * width),
            buf(block * seqs, cols * block),
            buf(cols * block, block * seqs),
            buf(width * seqs, block * ch),
            buf(block * seqs, width * ch),
            buf(block, j_len, ch),
            buf(sl, block, feat, dtype=F32),
            buf(width * width, ch, dtype=F32),
            buf(2 * width, feat, dtype=F32),
            buf(cols, block, LANES),
            buf(cols, block, LANES),
            buf(cols, j_len, LANES),
            buf(rows, block, LANES),
            buf(width, width, ch),
            buf(group, share, width, ch),
            buf(nz, share, width, ch),
            buf(group, share, width, ch),
            buf(group, part, LANES, dtype=F32),
            buf(group, part, LANES, dtype=F32),
            buf(nz, part, LANES, dtype=F32),
            buf(group, part, LANES, dtype=F32),
            pltpu.SemaphoreType.REGULAR,
            pltpu.SemaphoreType.DMA((7,)),
            pltpu.SemaphoreType.DMA((5,)),
            pltpu.SemaphoreType.DMA((11,)),
            pltpu.SemaphoreType.DMA((11,)),
        ],
        compiler_params=pltpu.CompilerParams(
            collective_id=0, has_side_effects=True, vmem_limit_bytes=56 * 1024 * 1024
        ),
        cost_estimate=pl.CostEstimate(
            flops=5_000_000_000, bytes_accessed=4_000_000, transcendentals=0
        ),
    )(
        x,
        we.T,
        gain.reshape(1, feat),
        shift.reshape(1, feat),
        eshift.reshape(1, 2 * width),
        fshift.reshape(1, ch),
        wf,
        g,
    )
    pair, align, ow, pw = pl.pallas_call(
        copy_kernel,
        out_shape=shapes,
        in_specs=[hbm] * 4,
        out_specs=[hbm] * 4,
        scratch_shapes=[pltpu.VMEM(v.shape, v.dtype) for v in shapes]
        + [pltpu.SemaphoreType.DMA((2, 16))],
        compiler_params=pltpu.CompilerParams(vmem_limit_bytes=56 * 1024 * 1024),
    )(*outs)
    return pair, align, ow, pw.T


def solution(mesh):
    in_specs = (P("col", "row", None), P(), P(), P(), P(), P(), P(), P("row", "col", None))
    out_specs = (P("row", "col", None), P("col", "row", None), P(), P())
    return jax.shard_map(
        on_device, mesh=mesh, in_specs=in_specs, out_specs=out_specs, check_vma=False
    )
```

```python
import functools

import jax
import jax.numpy as jnp
from jax import lax
from jax.experimental import pallas as pl
from jax.experimental.pallas import tpu as pltpu
from jax.sharding import PartitionSpec as P

BF16 = jnp.bfloat16
F32 = jnp.float32
MESH = pl.DeviceIdType.MESH
LANES = 128


def nt(x, y):
    return lax.dot_general(x, y, (((1,), (1,)), ((), ())), preferred_element_type=F32)


def nn(x, y):
    return lax.dot_general(x, y, (((1,), (0,)), ((), ())), preferred_element_type=F32)


def tn(x, y):
    return lax.dot_general(x, y, (((0,), (0,)), ((), ())), preferred_element_type=F32)


def iota(shape, dim):
    return lax.broadcasted_iota(jnp.int32, shape, dim)


def one_hot(cond):
    return jnp.where(cond, 1.0, 0.0).astype(BF16)


def wait_bytes(ref, sem):
    pltpu.make_async_copy(ref, ref, sem).wait()


def lane_aligned(start):
    return pl.multiple_of(start, LANES)


def kernel(
    rows,
    cols,
    x_hbm,
    we_hbm,
    gain_hbm,
    shift_hbm,
    eshift_hbm,
    fshift_hbm,
    wf_hbm,
    g_hbm,
    pair_hbm,
    align_hbm,
    ow_hbm,
    pw_hbm,
    x_ref,
    we_ref,
    gain_ref,
    shift_ref,
    eshift_ref,
    fshift_ref,
    wf_ref,
    a_all,
    b_all,
    b_piece,
    b_relay,
    gmat,
    wf32,
    w4,
    a_rows_ref,
    held,
    b_t,
    gather_rows,
    scatter_rows,
    aw,
    gp,
    pair_buf,
    align_buf,
    ow_buf,
    pw_buf,
    da_out,
    da_in,
    db_out,
    db_in,
    dw_out,
    dw_in,
    dw_mid,
    dw_fin,
    wg_out,
    wg_in,
    wg_mid,
    wg_fin,
    ready,
    in_sem,
    out_sem,
    send,
    recv,
):
    sl, block, feat = x_ref.shape
    width = we_ref.shape[0] // 2
    ch = wf_ref.shape[1]
    ratio = rows // cols
    seqs = sl * cols
    j_len = ratio * block
    inv_seq = 1.0 / seqs
    inv_res = 1.0 / (rows * block)
    me_r = lax.axis_index("row")
    me_c = lax.axis_index("col")
    near = cols // 2
    nz = rows // near
    y, z = me_r // nz, lax.rem(me_r, nz)
    x, core = me_c // 2, lax.rem(me_c, 2)
    group = near * cols
    member = y * cols + me_c

    def in_group(m):
        return ((m // cols) * nz + z, lax.rem(m, cols))

    def in_z(k):
        return (y * nz + k, me_c)

    barrier = pltpu.get_barrier_semaphore()

    def greet_group(k, carry):
        pl.semaphore_signal(
            barrier,
            inc=1,
            device_id=in_group(lax.rem(member + k, group)),
            device_id_type=MESH,
        )
        return carry

    def greet_z(k, carry):
        pl.semaphore_signal(
            barrier, inc=1, device_id=in_z(lax.rem(z + k, nz)), device_id_type=MESH
        )
        return carry

    loads = [
        pltpu.make_async_copy(src, dst, in_sem.at[k])
        for k, (src, dst) in enumerate(
            (
                (x_hbm, x_ref),
                (we_hbm, we_ref),
                (gain_hbm, gain_ref),
                (shift_hbm, shift_ref),
                (eshift_hbm, eshift_ref),
                (fshift_hbm, fshift_ref),
                (wf_hbm, wf_ref),
            )
        )
    ]
    for load in loads:
        load.start()
    lax.fori_loop(1, group, greet_group, 0)
    lax.fori_loop(1, nz, greet_z, 0)

    for i in range(block):
        pltpu.make_async_copy(
            g_hbm.at[i], gmat.at[:, pl.ds(i * ch, ch)], out_sem.at[0]
        ).start()

    loads[0].wait()
    xf = x_ref[...].astype(F32).reshape(sl * block, feat)
    centre = xf - jnp.mean(xf, axis=-1, keepdims=True)
    inv = lax.rsqrt(jnp.mean(centre * centre, axis=-1, keepdims=True) + 1e-05)
    normed = centre * inv
    for load in loads[1:-1]:
        load.wait()
    gain = gain_ref[...]
    lnout = (normed * gain + shift_ref[...]).astype(BF16)
    we = we_ref[...]
    we4 = jnp.concatenate([we[:width]] * sl + [we[width:]] * sl, axis=0)
    es = eshift_ref[...]
    es4 = jnp.concatenate([es[:, :width]] * sl + [es[:, width:]] * sl, axis=1)
    fshift = fshift_ref[...]
    proj = nt(lnout, we4) + es4
    owner_lane = (iota((block, 2 * LANES), 1) % LANES) // width
    piece = jnp.zeros((block, 2 * LANES), F32)
    for s in range(sl):
        piece = jnp.where(owner_lane == s, proj[s * block : (s + 1) * block], piece)
    piece = piece.astype(BF16)
    a_all[me_c] = piece[:, :LANES]
    b_piece[...] = piece[:, LANES:]

    pl.semaphore_wait(barrier, group - 1 + nz - 1)

    def send_all(count, peer_of, device_of, src, dst, phase):
        def body(k, carry):
            peer = peer_of(k)
            pltpu.make_async_remote_copy(
                src_ref=src(peer),
                dst_ref=dst,
                send_sem=send.at[phase],
                recv_sem=recv.at[phase],
                device_id=device_of(peer),
                device_id_type=MESH,
            ).start()
            return carry

        lax.fori_loop(1, count, body, 0)

    def to_cols(src, dst, phase):
        send_all(
            cols, lambda k: lax.rem(me_c + k, cols), lambda p: (me_r, p), src, dst, phase
        )

    def to_group(src, dst, phase):
        send_all(group, lambda k: lax.rem(member + k, group), in_group, src, dst, phase)

    def to_z(src, dst, phase):
        send_all(nz, lambda k: lax.rem(z + k, nz), in_z, src, dst, phase)

    to_cols(lambda peer: a_all.at[me_c], a_all.at[me_c], 0)
    relay = pltpu.make_async_remote_copy(
        src_ref=b_piece,
        dst_ref=b_relay,
        send_sem=send.at[1],
        recv_sem=recv.at[1],
        device_id=(x * nz + z, y * 2 + core),
        device_id_type=MESH,
    )

    @pl.when(x != y)
    def _():
        relay.start()

    @pl.when(x == y)
    def _():
        pltpu.make_async_copy(b_piece, b_relay, recv.at[1]).start()

    def confirm(k, carry):
        pl.semaphore_signal(
            ready,
            inc=1,
            device_id=in_group(lax.rem(member + k, group)),
            device_id_type=MESH,
        )
        return carry

    lax.fori_loop(1, group, confirm, 0)

    loads[-1].wait()
    wf32[...] = wf_ref[...].astype(F32)
    for e in range(width):
        block_e = wf32[pl.ds(e, width, stride=width), :].astype(BF16)
        for s in range(sl):
            w4[s * width : (s + 1) * width, e * ch : (e + 1) * ch] = block_e

    es_len = seqs * width
    is_len = block * seqs
    qi_len = block * cols
    at_row = iota((is_len, qi_len), 0)
    gather_rows[...] = one_hot(
        iota((is_len, qi_len), 1) == ((at_row % seqs) // sl) * block + at_row // seqs
    )
    at_lane = iota((qi_len, is_len), 1)
    scatter_rows[...] = one_hot(
        iota((qi_len, is_len), 0) == ((at_lane % seqs) // sl) * block + at_lane // seqs
    )
    own_seq = iota((is_len, LANES), 0) % sl == iota((is_len, LANES), 1) // width

    pl.semaphore_wait(ready, group - 1)
    wait_bytes(b_relay, recv.at[1])
    b_col = x * 2 + z // ratio
    b_slot = pl.ds(pl.multiple_of(lax.rem(z, ratio) * block, block), block)
    b_from = y * 2 + core

    def send_b(k, carry):
        peer = lax.rem(me_r + k, rows)
        own = jnp.logical_and(peer == me_r, b_col == me_c)

        @pl.when(jnp.logical_not(own))
        def _():
            pltpu.make_async_remote_copy(
                src_ref=b_relay,
                dst_ref=b_all.at[b_from, b_slot],
                send_sem=send.at[2],
                recv_sem=recv.at[2],
                device_id=(peer, b_col),
                device_id_type=MESH,
            ).start()

        @pl.when(own)
        def _():
            pltpu.make_async_copy(b_relay, b_all.at[b_from, b_slot], recv.at[2]).start()

        return carry

    lax.fori_loop(0, rows, send_b, 0)

    wait_bytes(a_all.at[pl.ds(0, cols - 1)], recv.at[0])
    a_cat = a_all[...].reshape(qi_len, LANES)
    a_rows_ref[...] = (jnp.where(own_seq, nn(gather_rows[...], a_cat), 0.0) * inv_seq).astype(
        BF16
    )
    chunk = min(256, is_len)
    lanes = 4 * ch

    def make_aw(m, carry):
        lhs = a_rows_ref[pl.ds(pl.multiple_of(m * chunk, chunk), chunk), :]
        per = chunk // seqs
        for n in range(width // 4):
            res = nn(lhs, w4[:, n * lanes : (n + 1) * lanes]).astype(BF16)
            for el in range(4):
                e = 4 * n + el
                for il in range(per):
                    at = pl.ds(lane_aligned((m * per + il) * ch), ch)
                    aw[e * seqs : (e + 1) * seqs, at] = res[
                        il * seqs : (il + 1) * seqs, el * ch : (el + 1) * ch
                    ]
        return carry

    lax.fori_loop(0, is_len // chunk, make_aw, 0, unroll=2)

    wait_bytes(gmat, out_sem.at[0])
    step = min(512, es_len)
    for n in range(0, es_len, step):
        held[n : n + step, :] = nt(aw[n : n + step, :], gmat[...])
    for q in range(cols):
        rows_q = [held[pl.ds(q * sl + s, width, stride=seqs), :] for s in range(sl)]
        db_out[q] = jnp.concatenate(rows_q, axis=0).T.astype(BF16)

    def send_db(t, carry):
        idx = lax.rem(t + me_r, rows)
        row_to = ratio * me_c + idx // cols
        col_to = idx % cols
        src = db_out.at[col_to, pl.ds(pl.multiple_of((idx // cols) * block, block), block)]
        own = jnp.logical_and(row_to == me_r, col_to == me_c)

        @pl.when(jnp.logical_not(own))
        def _():
            pltpu.make_async_remote_copy(
                src_ref=src,
                dst_ref=db_in.at[me_r],
                send_sem=send.at[3],
                recv_sem=recv.at[3],
                device_id=(row_to, col_to),
                device_id_type=MESH,
            ).start()

        @pl.when(own)
        def _():
            pltpu.make_async_copy(src, db_in.at[me_r], recv.at[3]).start()

        return carry

    lax.fori_loop(0, rows, send_db, 0)

    wait_bytes(b_all, recv.at[2])
    for q in range(cols):
        held[q * LANES : (q + 1) * LANES, :] = b_all[q].astype(F32).T
    for e in range(width):
        b_t[e * seqs : (e + 1) * seqs, :] = held[pl.ds(e, seqs, stride=width), :].astype(BF16)

    def make_g(m, carry):
        lhs = b_t[pl.ds(pl.multiple_of(m * chunk, chunk), chunk), :]
        per = chunk // seqs
        for n in range(block // 4):
            res = nn(lhs, gmat[:, n * lanes : (n + 1) * lanes]).astype(BF16)
            for il in range(4):
                i = 4 * n + il
                for el in range(per):
                    at = pl.ds(lane_aligned((m * per + el) * ch), ch)
                    gp[i * seqs : (i + 1) * seqs, at] = res[
                        el * seqs : (el + 1) * seqs, il * ch : (il + 1) * ch
                    ]
        return carry

    lax.fori_loop(0, es_len // chunk, make_g, 0, unroll=2)

    half = width // 2
    for h in range(2):
        res = tn(a_rows_ref[...], gp[:, h * half * ch : (h + 1) * half * ch])
        res = functools.reduce(
            lambda u, v: u + v, [res[s * width : (s + 1) * width] for s in range(sl)]
        ).astype(BF16)
        for el in range(half):
            dw_out[h * half + el] = res[:, el * ch : (el + 1) * ch]
    share = width // group
    to_group(lambda peer: dw_out.at[pl.ds(peer * share, share)], dw_in.at[member], 5)
    dw_in[member] = dw_out[pl.ds(member * share, share)]

    step = min(512, is_len)
    da_rows = jnp.concatenate(
        [nt(gp[n : n + step, :], w4[...]) * inv_seq for n in range(0, is_len, step)], axis=0
    )
    da_rows = jnp.where(own_seq, da_rows, 0.0).astype(BF16)
    da_out[...] = nn(scatter_rows[...], da_rows).astype(BF16).reshape(cols, block, LANES)
    to_cols(lambda peer: da_out.at[peer], da_in.at[me_c], 4)
    da_in[me_c] = da_out[me_c]

    b_es = jnp.concatenate(
        [b_t[n : n + LANES, :].T for n in range(0, es_len, LANES)], axis=1
    )
    half = block // 2
    for h in range(2):
        res = nn(b_es, aw[:, h * half * ch : (h + 1) * half * ch])
        for il in range(half):
            pair_buf[h * half + il] = (res[:, il * ch : (il + 1) * ch] + fshift).astype(BF16)
        at = pl.ds(h * half, half)
        pltpu.make_async_copy(pair_buf.at[at], pair_hbm.at[at], out_sem.at[1]).start()

    wait_bytes(da_in.at[pl.ds(0, cols - 1)], recv.at[4])
    wait_bytes(db_in, recv.at[3])
    da = jnp.sum(da_in[...].astype(F32), axis=0)
    db = jnp.sum(db_in[...].astype(F32), axis=0)
    dproj = jnp.concatenate([da, db], axis=1)
    dproj = jnp.concatenate(
        [jnp.where(owner_lane == s, dproj, 0.0) for s in range(sl)], axis=0
    )
    high = dproj.astype(BF16)
    low = (dproj - high.astype(F32)).astype(BF16)
    wg = tn(high, lnout) + tn(low, lnout)
    wg = jnp.concatenate(
        [
            functools.reduce(
                lambda u, v: u + v,
                [wg[h + s * width : h + (s + 1) * width] for s in range(sl)],
            )
            for h in (0, LANES)
        ],
        axis=0,
    )
    halves = feat // LANES
    part = halves * 2 * width // group
    for h in range(halves):
        for k in range(2 * width // part):
            wg_out[h * 2 * width // part + k] = wg[
                k * part : (k + 1) * part, h * LANES : (h + 1) * LANES
            ]
    to_group(lambda peer: wg_out.at[peer], wg_in.at[member], 8)
    wg_in[member] = wg_out[member]

    wait_bytes(dw_in.at[pl.ds(0, group - 1)], recv.at[5])
    dw_mid[z] = jnp.sum(dw_in[...].astype(F32), axis=0).astype(BF16)
    to_z(lambda peer: dw_mid.at[z], dw_mid.at[z], 6)

    dnorm = (nn(high, we4) + nn(low, we4)) * gain
    mean_one = jnp.mean(dnorm, axis=-1, keepdims=True)
    mean_two = jnp.mean(dnorm * normed, axis=-1, keepdims=True)
    align_buf[...] = (inv * (dnorm - mean_one - normed * mean_two)).reshape(sl, block, feat)
    align_copy = pltpu.make_async_copy(align_buf, align_hbm, out_sem.at[2])
    align_copy.start()

    wait_bytes(wg_in.at[pl.ds(0, group - 1)], recv.at[8])
    wg_mid[z] = jnp.sum(wg_in[...], axis=0)
    to_z(lambda peer: wg_mid.at[z], wg_mid.at[z], 9)

    wait_bytes(dw_mid.at[pl.ds(0, nz - 1)], recv.at[6])
    dw_fin[member] = (jnp.sum(dw_mid[...].astype(F32), axis=0) * inv_res).astype(BF16)
    to_group(lambda peer: dw_fin.at[member], dw_fin.at[member], 7)

    wait_bytes(wg_mid.at[pl.ds(0, nz - 1)], recv.at[9])
    wg_fin[member] = jnp.sum(wg_mid[...], axis=0) * inv_res
    to_group(lambda peer: wg_fin.at[member], wg_fin.at[member], 10)

    wait_bytes(dw_fin.at[pl.ds(0, group - 1)], recv.at[7])
    for m in range(group):
        for k in range(share):
            ow_buf[pl.ds(m * share + k, width, stride=width), :] = dw_fin[m, k].astype(F32)
    ow_copy = pltpu.make_async_copy(ow_buf, ow_hbm, out_sem.at[3])
    ow_copy.start()

    wait_bytes(wg_fin.at[pl.ds(0, group - 1)], recv.at[10])
    for h in range(halves):
        for k in range(2 * width // part):
            pw_buf[k * part : (k + 1) * part, h * LANES : (h + 1) * LANES] = wg_fin[
                h * 2 * width // part + k
            ]
    pw_copy = pltpu.make_async_copy(pw_buf, pw_hbm, out_sem.at[4])
    pw_copy.start()

    wait_bytes(a_all.at[pl.ds(0, cols - 1)], send.at[0])

    @pl.when(x != y)
    def _():
        relay.wait_send()

    @pl.when(b_col == me_c)
    def _():
        wait_bytes(db_in.at[pl.ds(0, rows - 1)], send.at[2])

    @pl.when(b_col != me_c)
    def _():
        wait_bytes(db_in, send.at[2])

    @pl.when(me_r // ratio == me_c)
    def _():
        wait_bytes(db_in.at[pl.ds(0, rows - 1)], send.at[3])

    @pl.when(me_r // ratio != me_c)
    def _():
        wait_bytes(db_in, send.at[3])

    wait_bytes(da_in.at[pl.ds(0, cols - 1)], send.at[4])
    wait_bytes(dw_in.at[pl.ds(0, group - 1)], send.at[5])
    wait_bytes(dw_mid.at[pl.ds(0, nz - 1)], send.at[6])
    wait_bytes(dw_fin.at[pl.ds(0, group - 1)], send.at[7])
    wait_bytes(wg_in.at[pl.ds(0, group - 1)], send.at[8])
    wait_bytes(wg_mid.at[pl.ds(0, nz - 1)], send.at[9])
    wait_bytes(wg_fin.at[pl.ds(0, group - 1)], send.at[10])
    wait_bytes(pair_buf, out_sem.at[1])
    align_copy.wait()
    ow_copy.wait()
    pw_copy.wait()


def copy_kernel(*refs):
    sem = refs[-1]
    parts = []
    for src, held, dst in zip(refs[0:4], refs[8:12], refs[4:8]):
        count = 4 if src.shape[0] * src.shape[1] >= 1024 else 1
        rows = src.shape[0] // count
        for k in range(count):
            at = pl.ds(k * rows, rows)
            n = len(parts)
            parts.append(
                (
                    pltpu.make_async_copy(src.at[at], held.at[at], sem.at[0, n]),
                    pltpu.make_async_copy(held.at[at], dst.at[at], sem.at[1, n]),
                )
            )
    for load, _ in parts:
        load.start()
    for load, store in parts:
        load.wait()
        store.start()
    for _, store in parts:
        store.wait()


def on_device(x, gain, shift, we, eshift, wf, fshift, g):
    rows = lax.axis_size("row")
    cols = lax.axis_size("col")
    sl, block, feat = x.shape
    width = we.shape[1] // 2
    ch = wf.shape[1]
    j_len = g.shape[1]
    seqs = sl * cols
    near = cols // 2
    nz = rows // near
    group = near * cols
    share = width // group
    part = feat * 2 * width // LANES // group
    hbm = pl.BlockSpec(memory_space=pl.ANY)

    def buf(*shape, dtype=BF16):
        return pltpu.VMEM(shape, dtype)

    shapes = [
        jax.ShapeDtypeStruct((block, j_len, ch), BF16),
        jax.ShapeDtypeStruct((sl, block, feat), F32),
        jax.ShapeDtypeStruct((width * width, ch), F32),
        jax.ShapeDtypeStruct((2 * width, feat), F32),
    ]
    outs = pl.pallas_call(
        functools.partial(kernel, rows, cols),
        out_shape=shapes,
        in_specs=[hbm] * 8,
        out_specs=[hbm] * 4,
        scratch_shapes=[
            buf(sl, block, feat),
            buf(2 * width, feat),
            buf(1, feat, dtype=F32),
            buf(1, feat, dtype=F32),
            buf(1, 2 * width, dtype=F32),
            buf(1, ch, dtype=F32),
            buf(width * width, ch),
            buf(cols, block, LANES),
            buf(cols, j_len, LANES),
            buf(block, LANES),
            buf(block, LANES),
            buf(j_len, block * ch),
            buf(width * width, ch, dtype=F32),
            buf(LANES, width * ch),
            buf(block * seqs, LANES),
            buf(seqs * width, j_len, dtype=F32),
            buf(seqs * width, j_len),
            buf(block * seqs, cols * block),
            buf(cols * block, block * seqs),
            buf(width * seqs, block * ch),
            buf(block * seqs, width * ch),
            buf(block, j_len, ch),
            buf(sl, block, feat, dtype=F32),
            buf(width * width, ch, dtype=F32),
            buf(2 * width, feat, dtype=F32),
            buf(cols, block, LANES),
            buf(cols, block, LANES),
            buf(cols, j_len, LANES),
            buf(rows, block, LANES),
            buf(width, width, ch),
            buf(group, share, width, ch),
            buf(nz, share, width, ch),
            buf(group, share, width, ch),
            buf(group, part, LANES, dtype=F32),
            buf(group, part, LANES, dtype=F32),
            buf(nz, part, LANES, dtype=F32),
            buf(group, part, LANES, dtype=F32),
            pltpu.SemaphoreType.REGULAR,
            pltpu.SemaphoreType.DMA((7,)),
            pltpu.SemaphoreType.DMA((5,)),
            pltpu.SemaphoreType.DMA((11,)),
            pltpu.SemaphoreType.DMA((11,)),
        ],
        compiler_params=pltpu.CompilerParams(
            collective_id=0, has_side_effects=True, vmem_limit_bytes=56 * 1024 * 1024
        ),
        cost_estimate=pl.CostEstimate(
            flops=5_000_000_000, bytes_accessed=4_000_000, transcendentals=0
        ),
    )(
        x,
        we.T,
        gain.reshape(1, feat),
        shift.reshape(1, feat),
        eshift.reshape(1, 2 * width),
        fshift.reshape(1, ch),
        wf,
        g,
    )
    pair, align, ow, pw = pl.pallas_call(
        copy_kernel,
        out_shape=shapes,
        in_specs=[hbm] * 4,
        out_specs=[hbm] * 4,
        scratch_shapes=[pltpu.VMEM(v.shape, v.dtype) for v in shapes]
        + [pltpu.SemaphoreType.DMA((2, 16))],
        compiler_params=pltpu.CompilerParams(vmem_limit_bytes=56 * 1024 * 1024),
    )(*outs)
    return pair, align, ow, pw.T


def solution(mesh):
    in_specs = (P("col", "row", None), P(), P(), P(), P(), P(), P(), P("row", "col", None))
    out_specs = (P("row", "col", None), P("col", "row", None), P(), P())
    return jax.shard_map(
        on_device, mesh=mesh, in_specs=in_specs, out_specs=out_specs, check_vma=False
    )
```

```python
import functools

import jax
import jax.numpy as jnp
from jax import lax
from jax.experimental import pallas as pl
from jax.experimental.pallas import tpu as pltpu
from jax.sharding import PartitionSpec as P

BF16 = jnp.bfloat16
F32 = jnp.float32
MESH = pl.DeviceIdType.MESH
LANES = 128


def nt(x, y):
    return lax.dot_general(x, y, (((1,), (1,)), ((), ())), preferred_element_type=F32)


def nn(x, y):
    return lax.dot_general(x, y, (((1,), (0,)), ((), ())), preferred_element_type=F32)


def tn(x, y):
    return lax.dot_general(x, y, (((0,), (0,)), ((), ())), preferred_element_type=F32)


def iota(shape, dim):
    return lax.broadcasted_iota(jnp.int32, shape, dim)


def one_hot(cond):
    return jnp.where(cond, 1.0, 0.0).astype(BF16)


def wait_bytes(ref, sem):
    pltpu.make_async_copy(ref, ref, sem).wait()


def lane_aligned(start):
    return pl.multiple_of(start, LANES)


def kernel(
    rows,
    cols,
    x_hbm,
    we_hbm,
    gain_hbm,
    shift_hbm,
    eshift_hbm,
    fshift_hbm,
    wf_hbm,
    g_hbm,
    pair_hbm,
    align_hbm,
    ow_hbm,
    pw_hbm,
    x_ref,
    we_ref,
    gain_ref,
    shift_ref,
    eshift_ref,
    fshift_ref,
    wf_ref,
    a_all,
    ln_all,
    b_all,
    b_piece,
    b_relay,
    gmat,
    wf32,
    w4,
    a_rows_ref,
    held,
    b_t,
    gather_rows,
    scatter_rows,
    aw,
    gp,
    pair_buf,
    align_buf,
    ow_buf,
    pw_buf,
    da_out,
    da_in,
    db_out,
    db_in,
    dw_out,
    dw_in,
    dw_mid,
    dw_fin,
    wg_out,
    wg_in,
    wg_mid,
    wg_fin,
    ready,
    in_sem,
    out_sem,
    send,
    recv,
):
    sl, block, feat = x_ref.shape
    width = we_ref.shape[0] // 2
    ch = wf_ref.shape[1]
    ratio = rows // cols
    seqs = sl * cols
    j_len = ratio * block
    inv_seq = 1.0 / seqs
    inv_res = 1.0 / (rows * block)
    me_r = lax.axis_index("row")
    me_c = lax.axis_index("col")
    near = cols // 2
    nz = rows // near
    y, z = me_r // nz, lax.rem(me_r, nz)
    x, core = me_c // 2, lax.rem(me_c, 2)
    group = near * cols
    member = y * cols + me_c

    ys = [lax.rem(y + k, near) for k in range(near)]
    cs = [lax.rem(me_c + k, cols) for k in range(cols)]
    zs = [lax.rem(z + k, nz) for k in range(nz)]

    def in_ring(k, size):
        return min(k, size - k)

    offsets = sorted(
        ((ky, kc) for ky in range(near) for kc in range(cols) if ky or kc),
        key=lambda o: -(in_ring(o[0], near) + in_ring((o[1] + 1) // 2, near)),
    )
    group_peers = [(ys[ky] * cols + cs[kc], (ys[ky] * nz + z, cs[kc])) for ky, kc in offsets]
    col_peers = [(cs[k], (me_r, cs[k])) for k in range(1, cols)]
    z_peers = [
        (zs[k], (y * nz + zs[k], me_c))
        for k in sorted(range(1, nz), key=lambda k: -in_ring(k, nz))
    ]

    relay_peers = [(x * nz + zs[k], y * 2 + core) for k in (1, nz - 1)]
    chip_peers = [lax.rem(x + k, near) * 2 + core for k in range(1, near)]
    sibling = (me_r, x * 2 + 1 - core)

    def in_group(m):
        return ((m // cols) * nz + z, m % cols)

    def in_z(k):
        return (y * nz + k, me_c)

    barrier = pltpu.get_barrier_semaphore()

    loads = [
        pltpu.make_async_copy(src, dst, in_sem.at[k])
        for k, (src, dst) in enumerate(
            (
                (x_hbm, x_ref),
                (we_hbm, we_ref),
                (gain_hbm, gain_ref),
                (shift_hbm, shift_ref),
                (eshift_hbm, eshift_ref),
                (fshift_hbm, fshift_ref),
                (wf_hbm, wf_ref),
            )
        )
    ]
    for load in loads:
        load.start()
    for device in relay_peers + [device for _, device in z_peers + group_peers]:
        pl.semaphore_signal(barrier, inc=1, device_id=device, device_id_type=MESH)

    for i in range(block):
        pltpu.make_async_copy(
            g_hbm.at[i], gmat.at[:, pl.ds(i * ch, ch)], out_sem.at[0]
        ).start()

    loads[0].wait()
    xf = x_ref[...].astype(F32).reshape(sl * block, feat)
    centre = xf - jnp.mean(xf, axis=-1, keepdims=True)
    inv = lax.rsqrt(jnp.mean(centre * centre, axis=-1, keepdims=True) + 1e-05)
    normed = centre * inv
    for load in loads[1:-1]:
        load.wait()
    gain = gain_ref[...]
    lnout = (normed * gain + shift_ref[...]).astype(BF16)
    ln_all[me_c] = lnout
    we = we_ref[...]
    we4 = jnp.concatenate([we[:width]] * sl + [we[width:]] * sl, axis=0)
    es = eshift_ref[...]
    es4 = jnp.concatenate([es[:, :width]] * sl + [es[:, width:]] * sl, axis=1)
    fshift = fshift_ref[...]
    proj = nt(lnout, we4) + es4
    owner_lane = (iota((block, 2 * LANES), 1) % LANES) // width
    piece = jnp.zeros((block, 2 * LANES), F32)
    for s in range(sl):
        piece = jnp.where(owner_lane == s, proj[s * block : (s + 1) * block], piece)
    piece = piece.astype(BF16)
    a_all[me_c] = piece[:, :LANES]
    b_piece[...] = piece[:, LANES:]

    pl.semaphore_wait(barrier, group - 1 + nz - 1 + 2)

    def remote(src, dst, phase, device, send_phase=None):
        return pltpu.make_async_remote_copy(
            src_ref=src,
            dst_ref=dst,
            send_sem=send.at[phase if send_phase is None else send_phase],
            recv_sem=recv.at[phase],
            device_id=device,
            device_id_type=MESH,
        )

    def to_peers(peers, src, dst, phase):
        for peer, device in peers:
            remote(src(peer), dst, phase, device).start()

    def to_cols(src, dst, phase):
        to_peers(col_peers, src, dst, phase)

    def to_group(src, dst, phase):
        to_peers(group_peers, src, dst, phase)

    def spread(peers, me, device_of, ref, phase):
        for peer in peers:

            @pl.when(me != peer)
            def _():
                remote(ref, ref, phase, device_of(peer)).start()

    group_order = sorted(
        range(group),
        key=lambda m: (in_ring(m // cols, near) + in_ring(m % cols // 2, near), -(m % 2)),
    )
    z_order = sorted(range(nz), key=lambda k: in_ring(k, nz))

    def spread_group(ref, phase):
        spread(group_order, member, in_group, ref, phase)

    def spread_z(ref, phase):
        spread(z_order, z, in_z, ref, phase)

    to_cols(lambda peer: a_all.at[me_c], a_all.at[me_c], 0)
    relays = [
        remote(b_piece, b_relay.at[k], 1, device) for k, device in enumerate(relay_peers)
    ]
    for relay in relays:
        relay.start()

    for _, device in group_peers:
        pl.semaphore_signal(ready, inc=1, device_id=device, device_id_type=MESH)

    loads[-1].wait()
    wf32[...] = wf_ref[...].astype(F32)
    for e in range(width):
        block_e = wf32[pl.ds(e, width, stride=width), :].astype(BF16)
        for s in range(sl):
            w4[s * width : (s + 1) * width, e * ch : (e + 1) * ch] = block_e

    es_len = seqs * width
    is_len = block * seqs
    qi_len = block * cols
    at_row = iota((is_len, qi_len), 0)
    gather_rows[...] = one_hot(
        iota((is_len, qi_len), 1) == ((at_row % seqs) // sl) * block + at_row // seqs
    )
    at_lane = iota((qi_len, is_len), 1)
    scatter_rows[...] = one_hot(
        iota((qi_len, is_len), 0) == ((at_lane % seqs) // sl) * block + at_lane // seqs
    )
    own_seq = iota((is_len, LANES), 0) % sl == iota((is_len, LANES), 1) // width

    wait_bytes(a_all.at[pl.ds(0, cols - 1)], recv.at[0])
    a_cat = a_all[...].reshape(qi_len, LANES)
    a_rows_ref[...] = (jnp.where(own_seq, nn(gather_rows[...], a_cat), 0.0) * inv_seq).astype(
        BF16
    )
    chunk = min(256, is_len)
    lanes = 4 * ch

    def make_aw(m):
        lhs = a_rows_ref[m * chunk : (m + 1) * chunk, :]
        per = chunk // seqs
        for n in range(width // 4):
            res = nn(lhs, w4[:, n * lanes : (n + 1) * lanes]).astype(BF16)
            for el in range(4):
                e = 4 * n + el
                for il in range(per):
                    i = m * per + il
                    aw[e * seqs : (e + 1) * seqs, i * ch : (i + 1) * ch] = res[
                        il * seqs : (il + 1) * seqs, el * ch : (el + 1) * ch
                    ]

    make_aw(0)

    pl.semaphore_wait(ready, group - 1)
    wait_bytes(b_relay, recv.at[1])
    b_from = y * 2 + core
    b_own = []
    for h, z_from in enumerate((zs[nz - 1], zs[1])):
        z_to = [lax.rem(z + nz - core - 2 * h + k, nz) for k in range(4)]
        b_col = x * 2 + z_from // ratio
        b_own.append(b_col == me_c)
        b_slot = pl.ds(pl.multiple_of(lax.rem(z_from, ratio) * block, block), block)
        src, dst = b_relay.at[h], b_all.at[b_from, b_slot]
        for ky in range(near):
            for kz in (3, 0, 2, 1):
                device = (ys[ky] * nz + z_to[kz], b_col)
                plane = remote(src, dst, 2, device, (2, 13)[h])
                if ky or kz not in ((0, 1), (2, 3))[h]:
                    plane.start()
                    continue
                own = jnp.logical_and(z_to[kz] == z, b_own[h])

                @pl.when(jnp.logical_not(own))
                def _():
                    plane.start()

                @pl.when(own)
                def _():
                    pltpu.make_async_copy(src, dst, recv.at[2]).start()

    for col in chip_peers:
        remote(ln_all.at[me_c], ln_all.at[me_c], 11, (me_r, col)).start()
    remote(ln_all.at[me_c], ln_all.at[me_c], 12, sibling).start()

    for m in range(1, is_len // chunk):
        make_aw(m)

    wait_bytes(gmat, out_sem.at[0])
    step = min(512, es_len)
    for n in range(0, es_len, step):
        held[n : n + step, :] = nt(aw[n : n + step, :], gmat[...])
    for q in range(cols):
        rows_q = [held[pl.ds(q * sl + s, width, stride=seqs), :] for s in range(sl)]
        db_out[q] = jnp.concatenate(rows_q, axis=0).T.astype(BF16)

    ks = [lax.rem(me_r // cols + k, ratio) for k in range(ratio)]
    ds = [lax.rem(me_r + k, cols) for k in range(cols)]
    for k_to in ks:
        for col_to in ds:
            row_to = ratio * me_c + k_to
            src = db_out.at[col_to, pl.ds(pl.multiple_of(k_to * block, block), block)]
            own = jnp.logical_and(row_to == me_r, col_to == me_c)

            @pl.when(jnp.logical_not(own))
            def _():
                remote(src, db_in.at[me_r], 3, (row_to, col_to)).start()

            @pl.when(own)
            def _():
                pltpu.make_async_copy(src, db_in.at[me_r], recv.at[3]).start()

    wait_bytes(ln_all.at[pl.ds(0, near - 1)], recv.at[11])
    for col in chip_peers:
        remote(ln_all.at[col], ln_all.at[col], 12, sibling).start()
    wait_bytes(b_all, recv.at[2])
    for q in range(cols):
        held[q * LANES : (q + 1) * LANES, :] = b_all[q].astype(F32).T
    for e in range(width):
        b_t[e * seqs : (e + 1) * seqs, :] = held[pl.ds(e, seqs, stride=width), :].astype(BF16)

    def make_g(m, carry):
        lhs = b_t[pl.ds(pl.multiple_of(m * chunk, chunk), chunk), :]
        per = chunk // seqs
        for n in range(block // 4):
            res = nn(lhs, gmat[:, n * lanes : (n + 1) * lanes]).astype(BF16)
            for il in range(4):
                i = 4 * n + il
                for el in range(per):
                    at = pl.ds(lane_aligned((m * per + el) * ch), ch)
                    gp[i * seqs : (i + 1) * seqs, at] = res[
                        el * seqs : (el + 1) * seqs, il * ch : (il + 1) * ch
                    ]
        return carry

    half = width // 2
    share = width // group
    chunks = es_len // chunk // 2
    for h in range(2):
        lax.fori_loop(h * chunks, (h + 1) * chunks, make_g, 0, unroll=chunks)
        res = tn(a_rows_ref[...], gp[:, h * half * ch : (h + 1) * half * ch])
        res = functools.reduce(
            lambda u, v: u + v, [res[s * width : (s + 1) * width] for s in range(sl)]
        ).astype(BF16)
        for el in range(half):
            dw_out[h * half + el] = res[:, el * ch : (el + 1) * ch]

        for k in range(group // 2):
            peer = h * (group // 2) + lax.rem(member + k, group // 2)

            @pl.when(peer != member)
            def _():
                src = dw_out.at[pl.ds(peer * share, share)]
                remote(src, dw_in.at[member], 5, in_group(peer)).start()

    dw_in[member] = dw_out[pl.ds(member * share, share)]

    step = min(512, is_len)
    da_rows = jnp.concatenate(
        [nt(gp[n : n + step, :], w4[...]) * inv_seq for n in range(0, is_len, step)], axis=0
    )
    da_rows = jnp.where(own_seq, da_rows, 0.0).astype(BF16)
    da_out[...] = nn(scatter_rows[...], da_rows).astype(BF16).reshape(cols, block, LANES)
    wait_bytes(ln_all.at[pl.ds(0, near)], recv.at[12])
    da_cat = da_out[...].reshape(qi_len, LANES)
    wg_a = [
        tn(da_cat, ln_all[:, s * block : (s + 1) * block, :].reshape(qi_len, feat))[
            s * width : (s + 1) * width
        ]
        for s in range(sl)
    ]

    def by_seq(v):
        lane_seq = iota(v.shape, 1) // width
        return jnp.concatenate([jnp.where(lane_seq == s, v, 0.0) for s in range(sl)], axis=0)

    def split(v):
        high = v.astype(BF16)
        return high, (v - high.astype(F32)).astype(BF16)

    wait_bytes(db_in, recv.at[3])
    db_high, db_low = split(by_seq(jnp.sum(db_in[...].astype(F32), axis=0)))
    wg_b = tn(db_high, lnout) + tn(db_low, lnout)
    wg_b = [wg_b[s * width : (s + 1) * width] for s in range(sl)]
    wg = jnp.concatenate([functools.reduce(lambda u, v: u + v, w) for w in (wg_a, wg_b)], axis=0)
    halves = feat // LANES
    part = halves * 2 * width // group
    for h in range(halves):
        for k in range(2 * width // part):
            wg_out[h * 2 * width // part + k] = wg[
                k * part : (k + 1) * part, h * LANES : (h + 1) * LANES
            ]
    to_group(lambda peer: wg_out.at[peer], wg_in.at[member], 8)
    wg_in[member] = wg_out[member]

    to_cols(lambda peer: da_out.at[peer], da_in.at[me_c], 4)
    da_in[me_c] = da_out[me_c]

    b_es = jnp.concatenate(
        [b_t[n : n + LANES, :].T for n in range(0, es_len, LANES)], axis=1
    )
    half = block // 2
    for h in range(2):
        res = nn(b_es, aw[:, h * half * ch : (h + 1) * half * ch])
        for il in range(half):
            pair_buf[h * half + il] = (res[:, il * ch : (il + 1) * ch] + fshift).astype(BF16)
        at = pl.ds(h * half, half)
        pltpu.make_async_copy(pair_buf.at[at], pair_hbm.at[at], out_sem.at[1]).start()

    wait_bytes(dw_in.at[pl.ds(0, group - 1)], recv.at[5])
    dw_mid[z] = jnp.sum(dw_in[...].astype(F32), axis=0).astype(BF16)
    spread_z(dw_mid.at[z], 6)

    wait_bytes(wg_in.at[pl.ds(0, group - 1)], recv.at[8])
    wg_mid[z] = jnp.sum(wg_in[...], axis=0)
    spread_z(wg_mid.at[z], 9)

    wait_bytes(dw_mid.at[pl.ds(0, nz - 1)], recv.at[6])
    dw_fin[member] = (jnp.sum(dw_mid[...].astype(F32), axis=0) * inv_res).astype(BF16)
    spread_group(dw_fin.at[member], 7)

    wait_bytes(da_in.at[pl.ds(0, cols - 1)], recv.at[4])
    da_high, da_low = split(by_seq(jnp.sum(da_in[...].astype(F32), axis=0)))
    dnorm = (
        nn(da_high, we4[:LANES])
        + nn(da_low, we4[:LANES])
        + nn(db_high, we4[LANES:])
        + nn(db_low, we4[LANES:])
    ) * gain
    mean_one = jnp.mean(dnorm, axis=-1, keepdims=True)
    mean_two = jnp.mean(dnorm * normed, axis=-1, keepdims=True)
    align_buf[...] = (inv * (dnorm - mean_one - normed * mean_two)).reshape(sl, block, feat)
    align_copy = pltpu.make_async_copy(align_buf, align_hbm, out_sem.at[2])
    align_copy.start()

    wait_bytes(wg_mid.at[pl.ds(0, nz - 1)], recv.at[9])
    wg_fin[member] = jnp.sum(wg_mid[...], axis=0) * inv_res
    spread_group(wg_fin.at[member], 10)

    wait_bytes(dw_fin.at[pl.ds(0, group - 1)], recv.at[7])
    for m in range(group):
        for k in range(share):
            ow_buf[pl.ds(m * share + k, width, stride=width), :] = dw_fin[m, k].astype(F32)
    ow_copy = pltpu.make_async_copy(ow_buf, ow_hbm, out_sem.at[3])
    ow_copy.start()

    wait_bytes(wg_fin.at[pl.ds(0, group - 1)], recv.at[10])
    for h in range(halves):
        for k in range(2 * width // part):
            pw_buf[k * part : (k + 1) * part, h * LANES : (h + 1) * LANES] = wg_fin[
                h * 2 * width // part + k
            ]
    pw_copy = pltpu.make_async_copy(pw_buf, pw_hbm, out_sem.at[4])
    pw_copy.start()

    wait_bytes(a_all.at[pl.ds(0, cols - 1)], send.at[0])

    wait_bytes(b_relay, send.at[1])
    for phase, own in zip((2, 13), b_own):

        @pl.when(own)
        def _():
            wait_bytes(db_in.at[pl.ds(0, rows // 2 - 1)], send.at[phase])

        @pl.when(jnp.logical_not(own))
        def _():
            wait_bytes(db_in.at[pl.ds(0, rows // 2)], send.at[phase])

    @pl.when(me_r // ratio == me_c)
    def _():
        wait_bytes(db_in.at[pl.ds(0, rows - 1)], send.at[3])

    @pl.when(me_r // ratio != me_c)
    def _():
        wait_bytes(db_in, send.at[3])

    wait_bytes(da_in.at[pl.ds(0, cols - 1)], send.at[4])
    wait_bytes(dw_in.at[pl.ds(0, group - 1)], send.at[5])
    wait_bytes(dw_mid.at[pl.ds(0, nz - 1)], send.at[6])
    wait_bytes(dw_fin.at[pl.ds(0, group - 1)], send.at[7])
    wait_bytes(wg_in.at[pl.ds(0, group - 1)], send.at[8])
    wait_bytes(wg_mid.at[pl.ds(0, nz - 1)], send.at[9])
    wait_bytes(wg_fin.at[pl.ds(0, group - 1)], send.at[10])
    wait_bytes(ln_all.at[pl.ds(0, near - 1)], send.at[11])
    wait_bytes(ln_all.at[pl.ds(0, near)], send.at[12])
    wait_bytes(pair_buf, out_sem.at[1])
    align_copy.wait()
    ow_copy.wait()
    pw_copy.wait()


def copy_kernel(*refs):
    sem = refs[8]
    copies = [pltpu.make_async_copy(refs[k], refs[4 + k], sem.at[k]) for k in range(4)]
    for copy in copies:
        copy.start()
    for copy in copies:
        copy.wait()


def on_device(x, gain, shift, we, eshift, wf, fshift, g):
    rows = lax.axis_size("row")
    cols = lax.axis_size("col")
    sl, block, feat = x.shape
    width = we.shape[1] // 2
    ch = wf.shape[1]
    j_len = g.shape[1]
    seqs = sl * cols
    near = cols // 2
    nz = rows // near
    group = near * cols
    share = width // group
    part = feat * 2 * width // LANES // group
    hbm = pl.BlockSpec(memory_space=pl.ANY)

    def buf(*shape, dtype=BF16):
        return pltpu.VMEM(shape, dtype)

    shapes = [
        jax.ShapeDtypeStruct((block, j_len, ch), BF16),
        jax.ShapeDtypeStruct((sl, block, feat), F32),
        jax.ShapeDtypeStruct((width * width, ch), F32),
        jax.ShapeDtypeStruct((2 * width, feat), F32),
    ]
    outs = pl.pallas_call(
        functools.partial(kernel, rows, cols),
        out_shape=shapes,
        in_specs=[hbm] * 8,
        out_specs=[hbm] * 4,
        scratch_shapes=[
            buf(sl, block, feat),
            buf(2 * width, feat),
            buf(1, feat, dtype=F32),
            buf(1, feat, dtype=F32),
            buf(1, 2 * width, dtype=F32),
            buf(1, ch, dtype=F32),
            buf(width * width, ch),
            buf(cols, block, LANES),
            buf(cols, sl * block, feat),
            buf(cols, j_len, LANES),
            buf(block, LANES),
            buf(2, block, LANES),
            buf(j_len, block * ch),
            buf(width * width, ch, dtype=F32),
            buf(LANES, width * ch),
            buf(block * seqs, LANES),
            buf(seqs * width, j_len, dtype=F32),
            buf(seqs * width, j_len),
            buf(block * seqs, cols * block),
            buf(cols * block, block * seqs),
            buf(width * seqs, block * ch),
            buf(block * seqs, width * ch),
            buf(block, j_len, ch),
            buf(sl, block, feat, dtype=F32),
            buf(width * width, ch, dtype=F32),
            buf(2 * width, feat, dtype=F32),
            buf(cols, block, LANES),
            buf(cols, block, LANES),
            buf(cols, j_len, LANES),
            buf(rows, block, LANES),
            buf(width, width, ch),
            buf(group, share, width, ch),
            buf(nz, share, width, ch),
            buf(group, share, width, ch),
            buf(group, part, LANES, dtype=F32),
            buf(group, part, LANES, dtype=F32),
            buf(nz, part, LANES, dtype=F32),
            buf(group, part, LANES, dtype=F32),
            pltpu.SemaphoreType.REGULAR,
            pltpu.SemaphoreType.DMA((7,)),
            pltpu.SemaphoreType.DMA((5,)),
            pltpu.SemaphoreType.DMA((14,)),
            pltpu.SemaphoreType.DMA((14,)),
        ],
        compiler_params=pltpu.CompilerParams(
            collective_id=0, has_side_effects=True, vmem_limit_bytes=34 * 1024 * 1024
        ),
        cost_estimate=pl.CostEstimate(
            flops=5_000_000_000, bytes_accessed=4_000_000, transcendentals=0
        ),
    )(
        *(
            pltpu.with_memory_space_constraint(v, pltpu.HBM)
            for v in (
                x,
                we.T,
                gain.reshape(1, feat),
                shift.reshape(1, feat),
                eshift.reshape(1, 2 * width),
                fshift.reshape(1, ch),
                wf,
                g,
            )
        )
    )
    pair, align, ow, pw = pl.pallas_call(
        copy_kernel,
        out_shape=shapes,
        in_specs=[hbm] * 4,
        out_specs=[hbm] * 4,
        scratch_shapes=[pltpu.SemaphoreType.DMA((4,))],
        compiler_params=pltpu.CompilerParams(vmem_limit_bytes=16 * 1024 * 1024),
    )(*outs)
    return pair, align, ow, pw.T


def solution(mesh):
    in_specs = (P("col", "row", None), P(), P(), P(), P(), P(), P(), P("row", "col", None))
    out_specs = (P("row", "col", None), P("col", "row", None), P(), P())
    return jax.shard_map(
        on_device, mesh=mesh, in_specs=in_specs, out_specs=out_specs, check_vma=False
    )
```

```python
import functools

import jax
import jax.numpy as jnp
from jax import lax
from jax.experimental import pallas as pl
from jax.experimental.pallas import tpu as pltpu
from jax.sharding import PartitionSpec as P

BF16 = jnp.bfloat16
F32 = jnp.float32
MESH = pl.DeviceIdType.MESH
LANES = 128


def nt(x, y):
    return lax.dot_general(x, y, (((1,), (1,)), ((), ())), preferred_element_type=F32)


def nn(x, y):
    return lax.dot_general(x, y, (((1,), (0,)), ((), ())), preferred_element_type=F32)


def tn(x, y):
    return lax.dot_general(x, y, (((0,), (0,)), ((), ())), preferred_element_type=F32)


def iota(shape, dim):
    return lax.broadcasted_iota(jnp.int32, shape, dim)


def one_hot(cond):
    return jnp.where(cond, 1.0, 0.0).astype(BF16)


def wait_bytes(ref, sem):
    pltpu.make_async_copy(ref, ref, sem).wait()


def lane_aligned(start):
    return pl.multiple_of(start, LANES)


def kernel(
    rows,
    cols,
    x_hbm,
    we_hbm,
    gain_hbm,
    shift_hbm,
    eshift_hbm,
    fshift_hbm,
    wf_hbm,
    g_hbm,
    pair_hbm,
    align_hbm,
    ow_hbm,
    pw_hbm,
    x_ref,
    we_ref,
    gain_ref,
    shift_ref,
    eshift_ref,
    fshift_ref,
    wf_ref,
    a_all,
    ln_all,
    ln_relay,
    b_all,
    b_piece,
    b_relay,
    gmat,
    wf32,
    w4,
    a_rows_ref,
    held,
    b_t,
    gather_rows,
    scatter_rows,
    aw,
    gp,
    pair_buf,
    align_buf,
    ow_buf,
    pw_buf,
    da_out,
    da_in,
    db_out,
    db_in,
    db_sum,
    db_fin,
    dw_out,
    dw_in,
    dw_mid,
    dw_fin,
    wg_out,
    wg_in,
    wg_mid,
    wg_fin,
    ready,
    in_sem,
    out_sem,
    send,
    recv,
):
    sl, block, feat = x_ref.shape
    width = we_ref.shape[0] // 2
    ch = wf_ref.shape[1]
    ratio = rows // cols
    seqs = sl * cols
    j_len = ratio * block
    inv_seq = 1.0 / seqs
    inv_res = 1.0 / (rows * block)
    me_r = lax.axis_index("row")
    me_c = lax.axis_index("col")
    near = cols // 2
    nz = rows // near
    y, z = me_r // nz, lax.rem(me_r, nz)
    x, core = me_c // 2, lax.rem(me_c, 2)
    group = near * cols
    member = y * cols + me_c

    ys = [lax.rem(y + k, near) for k in range(near)]
    cs = [lax.rem(me_c + k, cols) for k in range(cols)]
    zs = [lax.rem(z + k, nz) for k in range(nz)]

    def in_ring(k, size):
        return min(k, size - k)

    offsets = sorted(
        ((ky, kc) for ky in range(near) for kc in range(cols) if ky or kc),
        key=lambda o: -(in_ring(o[0], near) + in_ring((o[1] + 1) // 2, near)),
    )
    group_peers = [(ys[ky] * cols + cs[kc], (ys[ky] * nz + z, cs[kc])) for ky, kc in offsets]
    col_peers = [(cs[k], (me_r, cs[k])) for k in range(1, cols)]
    z_peers = [
        (zs[k], (y * nz + zs[k], me_c))
        for k in sorted(range(1, nz), key=lambda k: -in_ring(k, nz))
    ]

    relay_peers = [(x * nz + zs[k], y * 2 + core) for k in (1, nz - 1)]
    chip_peers = [lax.rem(x + k, near) * 2 + core for k in range(1, near)]
    z_near = [(y * nz + zs[k], me_c) for k in (1, nz - 1)]
    sibling = (me_r, x * 2 + 1 - core)

    def in_group(m):
        return ((m // cols) * nz + z, m % cols)

    def in_z(k):
        return (y * nz + k, me_c)

    barrier = pltpu.get_barrier_semaphore()

    loads = [
        pltpu.make_async_copy(src, dst, in_sem.at[k])
        for k, (src, dst) in enumerate(
            (
                (x_hbm, x_ref),
                (we_hbm, we_ref),
                (gain_hbm, gain_ref),
                (shift_hbm, shift_ref),
                (eshift_hbm, eshift_ref),
                (fshift_hbm, fshift_ref),
                (wf_hbm, wf_ref),
            )
        )
    ]
    for load in loads:
        load.start()
    for device in relay_peers + [device for _, device in z_peers + group_peers]:
        pl.semaphore_signal(barrier, inc=1, device_id=device, device_id_type=MESH)

    for i in range(block):
        pltpu.make_async_copy(
            g_hbm.at[i], gmat.at[:, pl.ds(i * ch, ch)], out_sem.at[0]
        ).start()

    loads[0].wait()
    xf = x_ref[...].astype(F32).reshape(sl * block, feat)
    centre = xf - jnp.mean(xf, axis=-1, keepdims=True)
    inv = lax.rsqrt(jnp.mean(centre * centre, axis=-1, keepdims=True) + 1e-05)
    normed = centre * inv
    for load in loads[1:-1]:
        load.wait()
    gain = gain_ref[...]
    lnout = (normed * gain + shift_ref[...]).astype(BF16)
    ln_all[me_c] = lnout
    we = we_ref[...]
    we4 = jnp.concatenate([we[:width]] * sl + [we[width:]] * sl, axis=0)
    es = eshift_ref[...]
    es4 = jnp.concatenate([es[:, :width]] * sl + [es[:, width:]] * sl, axis=1)
    fshift = fshift_ref[...]
    proj = nt(lnout, we4) + es4
    owner_lane = (iota((block, 2 * LANES), 1) % LANES) // width
    piece = jnp.zeros((block, 2 * LANES), F32)
    for s in range(sl):
        piece = jnp.where(owner_lane == s, proj[s * block : (s + 1) * block], piece)
    piece = piece.astype(BF16)
    a_all[me_c] = piece[:, :LANES]
    b_piece[...] = piece[:, LANES:]

    pl.semaphore_wait(barrier, group - 1 + nz - 1 + 2)

    def remote(src, dst, phase, device, send_phase=None):
        return pltpu.make_async_remote_copy(
            src_ref=src,
            dst_ref=dst,
            send_sem=send.at[phase if send_phase is None else send_phase],
            recv_sem=recv.at[phase],
            device_id=device,
            device_id_type=MESH,
        )

    def to_peers(peers, src, dst, phase):
        for peer, device in peers:
            remote(src(peer), dst, phase, device).start()

    def to_cols(src, dst, phase):
        to_peers(col_peers, src, dst, phase)

    def to_group(src, dst, phase):
        to_peers(group_peers, src, dst, phase)

    def spread(peers, me, device_of, ref, phase):
        for peer in peers:

            @pl.when(me != peer)
            def _():
                remote(ref, ref, phase, device_of(peer)).start()

    group_order = sorted(
        range(group),
        key=lambda m: (in_ring(m // cols, near) + in_ring(m % cols // 2, near), -(m % 2)),
    )
    z_order = sorted(range(nz), key=lambda k: in_ring(k, nz))

    def spread_group(ref, phase):
        spread(group_order, member, in_group, ref, phase)

    def spread_z(ref, phase):
        spread(z_order, z, in_z, ref, phase)

    relays = [
        remote(b_piece, b_relay.at[k], 1, device) for k, device in enumerate(relay_peers)
    ]
    for relay in relays:
        relay.start()
    to_cols(lambda peer: a_all.at[me_c], a_all.at[me_c], 0)

    for _, device in group_peers:
        pl.semaphore_signal(ready, inc=1, device_id=device, device_id_type=MESH)

    loads[-1].wait()
    wf32[...] = wf_ref[...].astype(F32)
    for e in range(width):
        block_e = wf32[pl.ds(e, width, stride=width), :].astype(BF16)
        for s in range(sl):
            w4[s * width : (s + 1) * width, e * ch : (e + 1) * ch] = block_e

    es_len = seqs * width
    is_len = block * seqs
    qi_len = block * cols
    at_row = iota((is_len, qi_len), 0)
    gather_rows[...] = one_hot(
        iota((is_len, qi_len), 1) == ((at_row % seqs) // sl) * block + at_row // seqs
    )
    at_lane = iota((qi_len, is_len), 1)
    scatter_rows[...] = one_hot(
        iota((qi_len, is_len), 0) == ((at_lane % seqs) // sl) * block + at_lane // seqs
    )
    own_seq = iota((is_len, LANES), 0) % sl == iota((is_len, LANES), 1) // width

    wait_bytes(a_all.at[pl.ds(0, cols - 1)], recv.at[0])
    a_cat = a_all[...].reshape(qi_len, LANES)
    a_rows_ref[...] = (jnp.where(own_seq, nn(gather_rows[...], a_cat), 0.0) * inv_seq).astype(
        BF16
    )
    chunk = min(256, is_len)
    lanes = 4 * ch

    def make_aw(m):
        lhs = a_rows_ref[m * chunk : (m + 1) * chunk, :]
        per = chunk // seqs
        for n in range(width // 4):
            res = nn(lhs, w4[:, n * lanes : (n + 1) * lanes]).astype(BF16)
            for el in range(4):
                e = 4 * n + el
                for il in range(per):
                    i = m * per + il
                    aw[e * seqs : (e + 1) * seqs, i * ch : (i + 1) * ch] = res[
                        il * seqs : (il + 1) * seqs, el * ch : (el + 1) * ch
                    ]

    make_aw(0)

    pl.semaphore_wait(ready, group - 1)
    wait_bytes(b_relay, recv.at[1])
    b_from = y * 2 + core
    b_own = []
    for h, z_from in enumerate((zs[nz - 1], zs[1])):
        z_to = [lax.rem(z + nz - core - 2 * h + k, nz) for k in range(4)]
        b_col = x * 2 + z_from // ratio
        b_own.append(b_col == me_c)
        b_slot = pl.ds(pl.multiple_of(lax.rem(z_from, ratio) * block, block), block)
        src, dst = b_relay.at[h], b_all.at[b_from, b_slot]
        for ky in sorted(range(near), key=lambda k: -in_ring(k, near)):
            for kz in (3, 0, 2, 1):
                device = (ys[ky] * nz + z_to[kz], b_col)
                plane = remote(src, dst, 2, device, (2, 13)[h])
                if ky or kz not in ((0, 1), (2, 3))[h]:
                    plane.start()
                    continue
                own = jnp.logical_and(z_to[kz] == z, b_own[h])

                @pl.when(jnp.logical_not(own))
                def _():
                    plane.start()

                @pl.when(own)
                def _():
                    pltpu.make_async_copy(src, dst, recv.at[2]).start()

    for col in chip_peers:
        remote(ln_all.at[me_c], ln_all.at[me_c], 11, (me_r, col)).start()
    remote(ln_all.at[me_c], ln_all.at[me_c], 12, sibling).start()

    for m in range(1, is_len // chunk):
        make_aw(m)

    wait_bytes(gmat, out_sem.at[0])
    step = min(512, es_len)
    for n in range(0, es_len, step):
        held[n : n + step, :] = nt(aw[n : n + step, :], gmat[...])
    for q in range(cols):
        rows_q = [held[pl.ds(q * sl + s, width, stride=seqs), :] for s in range(sl)]
        db_out[q] = jnp.concatenate(rows_q, axis=0).T.astype(BF16)

    for k in range(ratio):
        k_to = lax.rem(y + k, ratio)
        z_own = ratio * core + k_to
        for kc in range(2):
            c_to = lax.rem(kc + z // ratio, 2)
            turn = lax.rem(z - z_own - 1 + c_to + 2 * nz, nz)
            z_relay = lax.rem(z_own + 1 - 2 * (turn // 4) + nz, nz)
            for kx in range(near):
                x_to = lax.rem(x + z + kx, near)
                src = db_out.at[
                    x_to * 2 + c_to, pl.ds(pl.multiple_of(k_to * block, block), block)
                ]
                dst = db_in.at[turn * near + y]
                device = (x * nz + z_relay, x_to * 2 + c_to)
                own = jnp.logical_and(device[0] == me_r, device[1] == me_c)

                @pl.when(jnp.logical_not(own))
                def _():
                    remote(src, dst, 3, device).start()

                @pl.when(own)
                def _():
                    pltpu.make_async_copy(src, dst, recv.at[3]).start()

    for h, device in enumerate(z_near):
        remote(ln_all.at[me_c], ln_relay.at[h], 15, device).start()

    wait_bytes(ln_all.at[pl.ds(0, near - 1)], recv.at[11])
    for col in chip_peers:
        remote(ln_all.at[col], ln_all.at[col], 12, sibling).start()
    wait_bytes(b_all, recv.at[2])
    for q in range(cols):
        held[q * LANES : (q + 1) * LANES, :] = b_all[q].astype(F32).T
    for e in range(width):
        b_t[e * seqs : (e + 1) * seqs, :] = held[pl.ds(e, seqs, stride=width), :].astype(BF16)

    def make_g(m, carry):
        lhs = b_t[pl.ds(pl.multiple_of(m * chunk, chunk), chunk), :]
        per = chunk // seqs
        for n in range(block // 4):
            res = nn(lhs, gmat[:, n * lanes : (n + 1) * lanes]).astype(BF16)
            for il in range(4):
                i = 4 * n + il
                for el in range(per):
                    at = pl.ds(lane_aligned((m * per + el) * ch), ch)
                    gp[i * seqs : (i + 1) * seqs, at] = res[
                        el * seqs : (el + 1) * seqs, il * ch : (il + 1) * ch
                    ]
        return carry

    half = width // 2
    share = width // group
    chunks = es_len // chunk // 2
    for h in range(2):
        lax.fori_loop(h * chunks, (h + 1) * chunks, make_g, 0, unroll=chunks)
        res = tn(a_rows_ref[...], gp[:, h * half * ch : (h + 1) * half * ch])
        res = functools.reduce(
            lambda u, v: u + v, [res[s * width : (s + 1) * width] for s in range(sl)]
        ).astype(BF16)
        for el in range(half):
            dw_out[h * half + el] = res[:, el * ch : (el + 1) * ch]

        for k in range(group // 2):
            peer = h * (group // 2) + lax.rem(member + k, group // 2)

            @pl.when(peer != member)
            def _():
                src = dw_out.at[pl.ds(peer * share, share)]
                remote(src, dw_in.at[member], 5, in_group(peer)).start()

    dw_in[member] = dw_out[pl.ds(member * share, share)]

    step = min(512, is_len)
    da_rows = jnp.concatenate(
        [nt(gp[n : n + step, :], w4[...]) * inv_seq for n in range(0, is_len, step)], axis=0
    )
    da_rows = jnp.where(own_seq, da_rows, 0.0).astype(BF16)
    da_out[...] = nn(scatter_rows[...], da_rows).astype(BF16).reshape(cols, block, LANES)
    wait_bytes(ln_all.at[pl.ds(0, near)], recv.at[12])
    da_cat = da_out[...].reshape(qi_len, LANES)
    wg_a = [
        tn(da_cat, ln_all[:, s * block : (s + 1) * block, :].reshape(qi_len, feat))[
            s * width : (s + 1) * width
        ]
        for s in range(sl)
    ]

    def by_seq(v):
        lane_seq = iota(v.shape, 1) // width
        return jnp.concatenate([jnp.where(lane_seq == s, v, 0.0) for s in range(sl)], axis=0)

    def split(v):
        high = v.astype(BF16)
        return high, (v - high.astype(F32)).astype(BF16)

    wait_bytes(db_in, recv.at[3])
    wait_bytes(ln_relay, recv.at[15])
    wg_b = 0.0
    for h in range(2):
        db = jnp.sum(db_in[h * (rows // 2) : (h + 1) * (rows // 2)].astype(F32), axis=0)
        db_sum[h] = db.astype(BF16)
        wg_b += tn(by_seq(db).astype(BF16), ln_relay[h])
    wg_b = [wg_b[s * width : (s + 1) * width] for s in range(sl)]
    wg = jnp.concatenate([functools.reduce(lambda u, v: u + v, w) for w in (wg_a, wg_b)], axis=0)
    halves = feat // LANES
    part = halves * 2 * width // group
    for h in range(halves):
        for k in range(2 * width // part):
            wg_out[h * 2 * width // part + k] = wg[
                k * part : (k + 1) * part, h * LANES : (h + 1) * LANES
            ]
    to_group(lambda peer: wg_out.at[peer], wg_in.at[member], 8)
    wg_in[member] = wg_out[member]

    to_cols(lambda peer: da_out.at[peer], da_in.at[me_c], 4)
    da_in[me_c] = da_out[me_c]
    for h in range(2):
        remote(db_sum.at[h], db_fin.at[h], 16, z_near[1 - h]).start()

    b_es = jnp.concatenate(
        [b_t[n : n + LANES, :].T for n in range(0, es_len, LANES)], axis=1
    )
    half = block // 2
    for h in range(2):
        res = nn(b_es, aw[:, h * half * ch : (h + 1) * half * ch])
        for il in range(half):
            pair_buf[h * half + il] = (res[:, il * ch : (il + 1) * ch] + fshift).astype(BF16)
        at = pl.ds(h * half, half)
        pltpu.make_async_copy(pair_buf.at[at], pair_hbm.at[at], out_sem.at[1]).start()

    wait_bytes(dw_in.at[pl.ds(0, group - 1)], recv.at[5])
    dw_mid[z] = jnp.sum(dw_in[...].astype(F32), axis=0).astype(BF16)
    spread_z(dw_mid.at[z], 6)

    wait_bytes(wg_in.at[pl.ds(0, group - 1)], recv.at[8])
    wg_mid[z] = jnp.sum(wg_in[...], axis=0)
    spread_z(wg_mid.at[z], 9)

    wait_bytes(dw_mid.at[pl.ds(0, nz - 1)], recv.at[6])
    dw_fin[core, member // 2] = (jnp.sum(dw_mid[...].astype(F32), axis=0) * inv_res).astype(BF16)
    for chip in range(group // 2):

        @pl.when(member // 2 != chip)
        def _():
            own_part = dw_fin.at[core, member // 2]
            remote(own_part, own_part, 7, in_group(2 * chip + core)).start()


    wait_bytes(da_in.at[pl.ds(0, cols - 1)], recv.at[4])
    wait_bytes(db_fin, recv.at[16])
    db_high, db_low = split(by_seq(jnp.sum(db_fin[...].astype(F32), axis=0)))
    da_high, da_low = split(by_seq(jnp.sum(da_in[...].astype(F32), axis=0)))
    dnorm = (
        nn(da_high, we4[:LANES])
        + nn(da_low, we4[:LANES])
        + nn(db_high, we4[LANES:])
        + nn(db_low, we4[LANES:])
    ) * gain
    mean_one = jnp.mean(dnorm, axis=-1, keepdims=True)
    mean_two = jnp.mean(dnorm * normed, axis=-1, keepdims=True)
    align_buf[...] = (inv * (dnorm - mean_one - normed * mean_two)).reshape(sl, block, feat)
    align_copy = pltpu.make_async_copy(align_buf, align_hbm, out_sem.at[2])
    align_copy.start()

    wait_bytes(wg_mid.at[pl.ds(0, nz - 1)], recv.at[9])
    wg_fin[member] = jnp.sum(wg_mid[...], axis=0) * inv_res
    spread_group(wg_fin.at[member], 10)

    wait_bytes(dw_fin.at[0, pl.ds(0, group // 2 - 1)], recv.at[7])
    remote(dw_fin.at[core], dw_fin.at[core], 14, sibling).start()

    def put_dw(half):
        for chip in range(group // 2):
            for k in range(share):
                at = pl.ds((2 * chip + half) * share + k, width, stride=width)
                ow_buf[at, :] = dw_fin[half, chip, k].astype(F32)

    for half in range(2):
        pl.when(core == half)(functools.partial(put_dw, half))
    wait_bytes(dw_fin.at[0], recv.at[14])
    for half in range(2):
        pl.when(core != half)(functools.partial(put_dw, half))
    ow_copy = pltpu.make_async_copy(ow_buf, ow_hbm, out_sem.at[3])
    ow_copy.start()

    wait_bytes(wg_fin.at[pl.ds(0, group - 1)], recv.at[10])
    for h in range(halves):
        for k in range(2 * width // part):
            pw_buf[k * part : (k + 1) * part, h * LANES : (h + 1) * LANES] = wg_fin[
                h * 2 * width // part + k
            ]
    pw_copy = pltpu.make_async_copy(pw_buf, pw_hbm, out_sem.at[4])
    pw_copy.start()

    wait_bytes(a_all.at[pl.ds(0, cols - 1)], send.at[0])

    wait_bytes(b_relay, send.at[1])
    for phase, own in zip((2, 13), b_own):

        @pl.when(own)
        def _():
            wait_bytes(db_in.at[pl.ds(0, rows // 2 - 1)], send.at[phase])

        @pl.when(jnp.logical_not(own))
        def _():
            wait_bytes(db_in.at[pl.ds(0, rows // 2)], send.at[phase])

    own_count = jnp.where(
        x == y, b_own[0].astype(jnp.int32) + b_own[1].astype(jnp.int32), 0
    )
    for k in range(3):

        @pl.when(own_count == k)
        def _():
            wait_bytes(db_in.at[pl.ds(0, rows - k)], send.at[3])

    wait_bytes(ln_relay, send.at[15])
    wait_bytes(db_fin, send.at[16])
    wait_bytes(da_in.at[pl.ds(0, cols - 1)], send.at[4])
    wait_bytes(dw_in.at[pl.ds(0, group - 1)], send.at[5])
    wait_bytes(dw_mid.at[pl.ds(0, nz - 1)], send.at[6])
    wait_bytes(dw_fin.at[0, pl.ds(0, group // 2 - 1)], send.at[7])
    wait_bytes(dw_fin.at[0], send.at[14])
    wait_bytes(wg_in.at[pl.ds(0, group - 1)], send.at[8])
    wait_bytes(wg_mid.at[pl.ds(0, nz - 1)], send.at[9])
    wait_bytes(wg_fin.at[pl.ds(0, group - 1)], send.at[10])
    wait_bytes(ln_all.at[pl.ds(0, near - 1)], send.at[11])
    wait_bytes(ln_all.at[pl.ds(0, near)], send.at[12])
    wait_bytes(pair_buf, out_sem.at[1])
    align_copy.wait()
    ow_copy.wait()
    pw_copy.wait()


def copy_kernel(*refs):
    sem = refs[8]
    copies = [pltpu.make_async_copy(refs[k], refs[4 + k], sem.at[k]) for k in range(4)]
    for copy in copies:
        copy.start()
    for copy in copies:
        copy.wait()


def on_device(x, gain, shift, we, eshift, wf, fshift, g):
    rows = lax.axis_size("row")
    cols = lax.axis_size("col")
    sl, block, feat = x.shape
    width = we.shape[1] // 2
    ch = wf.shape[1]
    j_len = g.shape[1]
    seqs = sl * cols
    near = cols // 2
    nz = rows // near
    group = near * cols
    share = width // group
    part = feat * 2 * width // LANES // group
    hbm = pl.BlockSpec(memory_space=pl.ANY)

    def buf(*shape, dtype=BF16):
        return pltpu.VMEM(shape, dtype)

    shapes = [
        jax.ShapeDtypeStruct((block, j_len, ch), BF16),
        jax.ShapeDtypeStruct((sl, block, feat), F32),
        jax.ShapeDtypeStruct((width * width, ch), F32),
        jax.ShapeDtypeStruct((2 * width, feat), F32),
    ]
    outs = pl.pallas_call(
        functools.partial(kernel, rows, cols),
        out_shape=shapes,
        in_specs=[hbm] * 8,
        out_specs=[hbm] * 4,
        scratch_shapes=[
            buf(sl, block, feat),
            buf(2 * width, feat),
            buf(1, feat, dtype=F32),
            buf(1, feat, dtype=F32),
            buf(1, 2 * width, dtype=F32),
            buf(1, ch, dtype=F32),
            buf(width * width, ch),
            buf(cols, block, LANES),
            buf(cols, sl * block, feat),
            buf(2, sl * block, feat),
            buf(cols, j_len, LANES),
            buf(block, LANES),
            buf(2, block, LANES),
            buf(j_len, block * ch),
            buf(width * width, ch, dtype=F32),
            buf(LANES, width * ch),
            buf(block * seqs, LANES),
            buf(seqs * width, j_len, dtype=F32),
            buf(seqs * width, j_len),
            buf(block * seqs, cols * block),
            buf(cols * block, block * seqs),
            buf(width * seqs, block * ch),
            buf(block * seqs, width * ch),
            buf(block, j_len, ch),
            buf(sl, block, feat, dtype=F32),
            buf(width * width, ch, dtype=F32),
            buf(2 * width, feat, dtype=F32),
            buf(cols, block, LANES),
            buf(cols, block, LANES),
            buf(cols, j_len, LANES),
            buf(rows, block, LANES),
            buf(2, block, LANES),
            buf(2, block, LANES),
            buf(width, width, ch),
            buf(group, share, width, ch),
            buf(nz, share, width, ch),
            buf(2, group // 2, share, width, ch),
            buf(group, part, LANES, dtype=F32),
            buf(group, part, LANES, dtype=F32),
            buf(nz, part, LANES, dtype=F32),
            buf(group, part, LANES, dtype=F32),
            pltpu.SemaphoreType.REGULAR,
            pltpu.SemaphoreType.DMA((7,)),
            pltpu.SemaphoreType.DMA((5,)),
            pltpu.SemaphoreType.DMA((17,)),
            pltpu.SemaphoreType.DMA((17,)),
        ],
        compiler_params=pltpu.CompilerParams(
            collective_id=0, has_side_effects=True, vmem_limit_bytes=34 * 1024 * 1024
        ),
        cost_estimate=pl.CostEstimate(
            flops=5_000_000_000, bytes_accessed=4_000_000, transcendentals=0
        ),
    )(
        *(
            pltpu.with_memory_space_constraint(v, pltpu.HBM)
            for v in (
                x,
                we.T,
                gain.reshape(1, feat),
                shift.reshape(1, feat),
                eshift.reshape(1, 2 * width),
                fshift.reshape(1, ch),
                wf,
                g,
            )
        )
    )
    pair, align, ow, pw = pl.pallas_call(
        copy_kernel,
        out_shape=shapes,
        in_specs=[hbm] * 4,
        out_specs=[hbm] * 4,
        scratch_shapes=[pltpu.SemaphoreType.DMA((4,))],
        compiler_params=pltpu.CompilerParams(vmem_limit_bytes=16 * 1024 * 1024),
    )(*outs)
    return pair, align, ow, pw.T


def solution(mesh):
    in_specs = (P("col", "row", None), P(), P(), P(), P(), P(), P(), P("row", "col", None))
    out_specs = (P("row", "col", None), P("col", "row", None), P(), P())
    return jax.shard_map(
        on_device, mesh=mesh, in_specs=in_specs, out_specs=out_specs, check_vma=False
    )
```

```python
import functools

import jax
import jax.numpy as jnp
from jax import lax
from jax.experimental import pallas as pl
from jax.experimental.pallas import tpu as pltpu
from jax.sharding import PartitionSpec as P

BF16 = jnp.bfloat16
F32 = jnp.float32
MESH = pl.DeviceIdType.MESH
LANES = 128


def nt(x, y):
    return lax.dot_general(x, y, (((1,), (1,)), ((), ())), preferred_element_type=F32)


def nn(x, y):
    return lax.dot_general(x, y, (((1,), (0,)), ((), ())), preferred_element_type=F32)


def tn(x, y):
    return lax.dot_general(x, y, (((0,), (0,)), ((), ())), preferred_element_type=F32)


def iota(shape, dim):
    return lax.broadcasted_iota(jnp.int32, shape, dim)


def one_hot(cond):
    return jnp.where(cond, 1.0, 0.0).astype(BF16)


def wait_bytes(ref, sem):
    pltpu.make_async_copy(ref, ref, sem).wait()


def lane_aligned(start):
    return pl.multiple_of(start, LANES)


def kernel(
    rows,
    cols,
    x_hbm,
    we_hbm,
    gain_hbm,
    shift_hbm,
    eshift_hbm,
    fshift_hbm,
    wf_hbm,
    g_hbm,
    pair_hbm,
    align_hbm,
    ow_hbm,
    pw_hbm,
    x_ref,
    we_ref,
    gain_ref,
    shift_ref,
    eshift_ref,
    fshift_ref,
    wf_ref,
    a_all,
    ln_all,
    ln_relay,
    b_all,
    b_piece,
    b_relay,
    gmat,
    wf32,
    w4,
    a_rows_ref,
    held,
    b_t,
    gather_rows,
    scatter_rows,
    aw,
    gp,
    pair_buf,
    align_buf,
    ow_buf,
    pw_buf,
    da_out,
    da_in,
    db_out,
    db_in,
    db_sum,
    db_fin,
    dw_out,
    dw_in,
    dw_mid,
    dw_fin,
    wg_out,
    wg_in,
    wg_mid,
    wg_fin,
    ready,
    in_sem,
    out_sem,
    send,
    recv,
):
    sl, block, feat = x_ref.shape
    width = we_ref.shape[0] // 2
    ch = wf_ref.shape[1]
    ratio = rows // cols
    seqs = sl * cols
    j_len = ratio * block
    inv_seq = 1.0 / seqs
    inv_res = 1.0 / (rows * block)
    me_r = lax.axis_index("row")
    me_c = lax.axis_index("col")
    near = cols // 2
    nz = rows // near
    y, z = me_r // nz, lax.rem(me_r, nz)
    x, core = me_c // 2, lax.rem(me_c, 2)
    group = near * cols
    member = y * cols + me_c

    ys = [lax.rem(y + k, near) for k in range(near)]
    cs = [lax.rem(me_c + k, cols) for k in range(cols)]
    zs = [lax.rem(z + k, nz) for k in range(nz)]

    def in_ring(k, size):
        return min(k, size - k)

    offsets = sorted(
        ((ky, kc) for ky in range(near) for kc in range(cols) if ky or kc),
        key=lambda o: -(in_ring(o[0], near) + in_ring((o[1] + 1) // 2, near)),
    )
    group_peers = [(ys[ky] * cols + cs[kc], (ys[ky] * nz + z, cs[kc])) for ky, kc in offsets]
    col_peers = [(cs[k], (me_r, cs[k])) for k in range(1, cols)]
    z_peers = [
        (zs[k], (y * nz + zs[k], me_c))
        for k in sorted(range(1, nz), key=lambda k: -in_ring(k, nz))
    ]

    turned = [lax.rem(v + near // 2, near) for v in (x, y)]
    relay_peers = [
        (v * nz + zs[k], y * 2 + core) for v in (x, turned[0]) for k in (1, nz - 1)
    ]
    relay_sources = [
        (x * nz + zs[k], v * 2 + core) for v in (y, turned[1]) for k in (1, nz - 1)
    ]
    chip_peers = [lax.rem(x + k, near) * 2 + core for k in range(1, near)]
    z_near = [(y * nz + zs[k], me_c) for k in (1, nz - 1)]
    sibling = (me_r, x * 2 + 1 - core)

    def in_group(m):
        return ((m // cols) * nz + z, m % cols)

    def in_z(k):
        return (y * nz + k, me_c)

    barrier = pltpu.get_barrier_semaphore()

    loads = [
        pltpu.make_async_copy(src, dst, in_sem.at[k])
        for k, (src, dst) in enumerate(
            (
                (x_hbm, x_ref),
                (we_hbm, we_ref),
                (gain_hbm, gain_ref),
                (shift_hbm, shift_ref),
                (eshift_hbm, eshift_ref),
                (fshift_hbm, fshift_ref),
                (wf_hbm, wf_ref),
            )
        )
    ]
    loads[0].start()
    loads[1].start()
    for device in relay_sources + [device for _, device in z_peers + group_peers]:
        pl.semaphore_signal(barrier, inc=1, device_id=device, device_id_type=MESH)
    for load in loads[2:]:
        load.start()

    for i in range(block):
        pltpu.make_async_copy(
            g_hbm.at[i], gmat.at[:, pl.ds(i * ch, ch)], out_sem.at[0]
        ).start()

    loads[0].wait()
    xf = x_ref[...].astype(F32).reshape(sl * block, feat)
    centre = xf - jnp.mean(xf, axis=-1, keepdims=True)
    inv = lax.rsqrt(jnp.mean(centre * centre, axis=-1, keepdims=True) + 1e-05)
    normed = centre * inv
    for load in loads[1:-1]:
        load.wait()
    gain = gain_ref[...]
    lnout = (normed * gain + shift_ref[...]).astype(BF16)
    ln_all[me_c] = lnout
    we = we_ref[...]
    we4 = jnp.concatenate([we[:width]] * sl + [we[width:]] * sl, axis=0)
    es = eshift_ref[...]
    es4 = jnp.concatenate([es[:, :width]] * sl + [es[:, width:]] * sl, axis=1)
    fshift = fshift_ref[...]
    proj = nt(lnout, we4) + es4
    owner_lane = (iota((block, 2 * LANES), 1) % LANES) // width
    piece = jnp.zeros((block, 2 * LANES), F32)
    for s in range(sl):
        piece = jnp.where(owner_lane == s, proj[s * block : (s + 1) * block], piece)
    piece = piece.astype(BF16)
    a_all[me_c] = piece[:, :LANES]
    b_piece[...] = piece[:, LANES:]

    pl.semaphore_wait(barrier, group - 1 + nz - 1 + 4)

    def remote(src, dst, phase, device, send_phase=None):
        return pltpu.make_async_remote_copy(
            src_ref=src,
            dst_ref=dst,
            send_sem=send.at[phase if send_phase is None else send_phase],
            recv_sem=recv.at[phase],
            device_id=device,
            device_id_type=MESH,
        )

    def to_peers(peers, src, dst, phase):
        for peer, device in peers:
            remote(src(peer), dst, phase, device).start()

    def to_cols(src, dst, phase):
        to_peers(col_peers, src, dst, phase)

    def to_group(src, dst, phase):
        to_peers(group_peers, src, dst, phase)

    def spread(peers, me, device_of, ref, phase):
        for peer in peers:

            @pl.when(me != peer)
            def _():
                remote(ref, ref, phase, device_of(peer)).start()

    group_order = sorted(
        range(group),
        key=lambda m: (in_ring(m // cols, near) + in_ring(m % cols // 2, near), -(m % 2)),
    )
    z_order = sorted(range(nz), key=lambda k: in_ring(k, nz))

    def spread_group(ref, phase):
        spread(group_order, member, in_group, ref, phase)

    def spread_z(ref, phase):
        spread(z_order, z, in_z, ref, phase)

    to_cols(lambda peer: a_all.at[me_c], a_all.at[me_c], 0)
    relays = [
        remote(b_piece, b_relay.at[k], 1, device) for k, device in enumerate(relay_peers)
    ]
    for relay in relays:
        relay.start()

    for _, device in group_peers:
        pl.semaphore_signal(ready, inc=1, device_id=device, device_id_type=MESH)

    loads[-1].wait()
    wf32[...] = wf_ref[...].astype(F32)
    for e in range(width):
        block_e = wf32[pl.ds(e, width, stride=width), :].astype(BF16)
        for s in range(sl):
            w4[s * width : (s + 1) * width, e * ch : (e + 1) * ch] = block_e

    es_len = seqs * width
    is_len = block * seqs
    qi_len = block * cols
    at_row = iota((is_len, qi_len), 0)
    gather_rows[...] = one_hot(
        iota((is_len, qi_len), 1) == ((at_row % seqs) // sl) * block + at_row // seqs
    )
    at_lane = iota((qi_len, is_len), 1)
    scatter_rows[...] = one_hot(
        iota((qi_len, is_len), 0) == ((at_lane % seqs) // sl) * block + at_lane // seqs
    )
    own_seq = iota((is_len, LANES), 0) % sl == iota((is_len, LANES), 1) // width

    wait_bytes(a_all.at[pl.ds(0, cols - 1)], recv.at[0])
    a_cat = a_all[...].reshape(qi_len, LANES)
    a_rows_ref[...] = (jnp.where(own_seq, nn(gather_rows[...], a_cat), 0.0) * inv_seq).astype(
        BF16
    )
    chunk = min(256, is_len)
    lanes = 4 * ch

    def make_aw(m):
        lhs = a_rows_ref[m * chunk : (m + 1) * chunk, :]
        per = chunk // seqs
        for n in range(width // 4):
            res = nn(lhs, w4[:, n * lanes : (n + 1) * lanes]).astype(BF16)
            for el in range(4):
                e = 4 * n + el
                for il in range(per):
                    i = m * per + il
                    aw[e * seqs : (e + 1) * seqs, i * ch : (i + 1) * ch] = res[
                        il * seqs : (il + 1) * seqs, el * ch : (el + 1) * ch
                    ]

    make_aw(0)

    pl.semaphore_wait(ready, group - 1)
    wait_bytes(b_relay, recv.at[1])
    b_own = []
    y_to = [y, lax.rem(y + 1 + 2 * core, near)]
    for h, z_from in enumerate((zs[nz - 1], zs[1])):
        z_to = [lax.rem(z + nz - core - 2 * h + k, nz) for k in range(4)]
        b_col = x * 2 + z_from // ratio
        b_own.append(b_col == me_c)
        b_slot = pl.ds(pl.multiple_of(lax.rem(z_from, ratio) * block, block), block)
        for ky in (1, 0):
            for kz in (3, 0, 2, 1):
                for v, x_from in enumerate((y, turned[1])):
                    src, dst = b_relay.at[2 * v + h], b_all.at[x_from * 2 + core, b_slot]
                    device = (y_to[ky] * nz + z_to[kz], b_col)
                    plane = remote(src, dst, 2, device, (2, 13)[h])
                    if ky or kz not in ((0, 1), (2, 3))[h]:
                        plane.start()
                        continue
                    own = jnp.logical_and(z_to[kz] == z, b_own[h])

                    @pl.when(jnp.logical_not(own))
                    def _():
                        plane.start()

                    @pl.when(own)
                    def _():
                        pltpu.make_async_copy(src, dst, recv.at[2]).start()

    for col in chip_peers:
        remote(ln_all.at[me_c], ln_all.at[me_c], 11, (me_r, col)).start()
    remote(ln_all.at[me_c], ln_all.at[me_c], 12, sibling).start()

    for m in range(1, is_len // chunk):
        make_aw(m)

    wait_bytes(gmat, out_sem.at[0])
    step = min(512, es_len)
    for n in range(0, es_len, step):
        held[n : n + step, :] = nt(aw[n : n + step, :], gmat[...])
    for q in range(cols):
        rows_q = [held[pl.ds(q * sl + s, width, stride=seqs), :] for s in range(sl)]
        db_out[q] = jnp.concatenate(rows_q, axis=0).T.astype(BF16)

    for k in range(ratio):
        k_to = lax.rem(y + k, ratio)
        z_own = ratio * core + k_to
        for kc in range(2):
            c_to = lax.rem(kc + z // ratio, 2)
            turn = lax.rem(z - z_own - 1 + c_to + 2 * nz, nz)
            z_relay = lax.rem(z_own + 1 - 2 * (turn // 4) + nz, nz)
            for kx in range(near):
                x_to = lax.rem(x + z + kx, near)
                src = db_out.at[
                    x_to * 2 + c_to, pl.ds(pl.multiple_of(k_to * block, block), block)
                ]
                dst = db_in.at[turn * near + y]
                device = (x * nz + z_relay, x_to * 2 + c_to)
                own = jnp.logical_and(device[0] == me_r, device[1] == me_c)

                @pl.when(jnp.logical_not(own))
                def _():
                    remote(src, dst, 3, device).start()

                @pl.when(own)
                def _():
                    pltpu.make_async_copy(src, dst, recv.at[3]).start()

    for h, device in enumerate(z_near):
        remote(ln_all.at[me_c], ln_relay.at[h], 15, device).start()

    wait_bytes(ln_all.at[pl.ds(0, near - 1)], recv.at[11])
    for col in chip_peers:
        remote(ln_all.at[col], ln_all.at[col], 12, sibling).start()
    wait_bytes(b_all, recv.at[2])
    for q in range(cols):
        held[q * LANES : (q + 1) * LANES, :] = b_all[q].astype(F32).T
    for e in range(width):
        b_t[e * seqs : (e + 1) * seqs, :] = held[pl.ds(e, seqs, stride=width), :].astype(BF16)

    def make_g(m, carry):
        lhs = b_t[pl.ds(pl.multiple_of(m * chunk, chunk), chunk), :]
        per = chunk // seqs
        for n in range(block // 4):
            res = nn(lhs, gmat[:, n * lanes : (n + 1) * lanes]).astype(BF16)
            for il in range(4):
                i = 4 * n + il
                for el in range(per):
                    at = pl.ds(lane_aligned((m * per + el) * ch), ch)
                    gp[i * seqs : (i + 1) * seqs, at] = res[
                        el * seqs : (el + 1) * seqs, il * ch : (il + 1) * ch
                    ]
        return carry

    half = width // 2
    share = width // group
    chunks = es_len // chunk // 2
    for h in range(2):
        lax.fori_loop(h * chunks, (h + 1) * chunks, make_g, 0, unroll=chunks)
        res = tn(a_rows_ref[...], gp[:, h * half * ch : (h + 1) * half * ch])
        res = functools.reduce(
            lambda u, v: u + v, [res[s * width : (s + 1) * width] for s in range(sl)]
        ).astype(BF16)
        for el in range(half):
            dw_out[h * half + el] = res[:, el * ch : (el + 1) * ch]

        for k in range(group // 2):
            peer = h * (group // 2) + lax.rem(member + k, group // 2)

            @pl.when(peer != member)
            def _():
                src = dw_out.at[pl.ds(peer * share, share)]
                remote(src, dw_in.at[member], 5, in_group(peer)).start()

    dw_in[member] = dw_out[pl.ds(member * share, share)]

    step = min(512, is_len)
    da_rows = jnp.concatenate(
        [nt(gp[n : n + step, :], w4[...]) * inv_seq for n in range(0, is_len, step)], axis=0
    )
    da_rows = jnp.where(own_seq, da_rows, 0.0).astype(BF16)
    da_out[...] = nn(scatter_rows[...], da_rows).astype(BF16).reshape(cols, block, LANES)
    wait_bytes(ln_all.at[pl.ds(0, near)], recv.at[12])
    da_cat = da_out[...].reshape(qi_len, LANES)
    wg_a = [
        tn(da_cat, ln_all[:, s * block : (s + 1) * block, :].reshape(qi_len, feat))[
            s * width : (s + 1) * width
        ]
        for s in range(sl)
    ]

    def by_seq(v):
        lane_seq = iota(v.shape, 1) // width
        return jnp.concatenate([jnp.where(lane_seq == s, v, 0.0) for s in range(sl)], axis=0)

    def split(v):
        high = v.astype(BF16)
        return high, (v - high.astype(F32)).astype(BF16)

    wait_bytes(db_in, recv.at[3])
    wait_bytes(ln_relay, recv.at[15])
    wg_b = 0.0
    for h in range(2):
        db = jnp.sum(db_in[h * (rows // 2) : (h + 1) * (rows // 2)].astype(F32), axis=0)
        db_sum[h] = db.astype(BF16)
        wg_b += tn(by_seq(db).astype(BF16), ln_relay[h])
    wg_b = [wg_b[s * width : (s + 1) * width] for s in range(sl)]
    wg = jnp.concatenate([functools.reduce(lambda u, v: u + v, w) for w in (wg_a, wg_b)], axis=0)
    halves = feat // LANES
    part = halves * 2 * width // group
    for h in range(halves):
        for k in range(2 * width // part):
            wg_out[h * 2 * width // part + k] = wg[
                k * part : (k + 1) * part, h * LANES : (h + 1) * LANES
            ]
    to_group(lambda peer: wg_out.at[peer], wg_in.at[member], 8)
    wg_in[member] = wg_out[member]

    wait_bytes(dw_in.at[pl.ds(0, group - 1)], recv.at[5])
    dw_mid[z] = jnp.sum(dw_in[...].astype(F32), axis=0).astype(BF16)
    spread_z(dw_mid.at[z], 6)

    to_cols(lambda peer: da_out.at[peer], da_in.at[me_c], 4)
    da_in[me_c] = da_out[me_c]
    for h in range(2):
        remote(db_sum.at[h], db_fin.at[h], 16, z_near[1 - h]).start()

    b_es = jnp.concatenate(
        [b_t[n : n + LANES, :].T for n in range(0, es_len, LANES)], axis=1
    )
    half = block // 2
    for h in range(2):
        res = nn(b_es, aw[:, h * half * ch : (h + 1) * half * ch])
        for il in range(half):
            pair_buf[h * half + il] = (res[:, il * ch : (il + 1) * ch] + fshift).astype(BF16)
        at = pl.ds(h * half, half)
        pltpu.make_async_copy(pair_buf.at[at], pair_hbm.at[at], out_sem.at[1]).start()

    wait_bytes(wg_in.at[pl.ds(0, group - 1)], recv.at[8])
    wg_mid[z] = jnp.sum(wg_in[...], axis=0)
    spread_z(wg_mid.at[z], 9)

    wait_bytes(dw_mid.at[pl.ds(0, nz - 1)], recv.at[6])
    dw_fin[core, member // 2] = (jnp.sum(dw_mid[...].astype(F32), axis=0) * inv_res).astype(BF16)
    for chip in range(group // 2):

        @pl.when(member // 2 != chip)
        def _():
            own_part = dw_fin.at[core, member // 2]
            remote(own_part, own_part, 7, in_group(2 * chip + core)).start()


    wait_bytes(da_in.at[pl.ds(0, cols - 1)], recv.at[4])
    wait_bytes(db_fin, recv.at[16])
    db_high, db_low = split(by_seq(jnp.sum(db_fin[...].astype(F32), axis=0)))
    da_high, da_low = split(by_seq(jnp.sum(da_in[...].astype(F32), axis=0)))
    dnorm = (
        nn(da_high, we4[:LANES])
        + nn(da_low, we4[:LANES])
        + nn(db_high, we4[LANES:])
        + nn(db_low, we4[LANES:])
    ) * gain
    mean_one = jnp.mean(dnorm, axis=-1, keepdims=True)
    mean_two = jnp.mean(dnorm * normed, axis=-1, keepdims=True)
    align_buf[...] = (inv * (dnorm - mean_one - normed * mean_two)).reshape(sl, block, feat)
    align_copy = pltpu.make_async_copy(align_buf, align_hbm, out_sem.at[2])
    align_copy.start()

    wait_bytes(wg_mid.at[pl.ds(0, nz - 1)], recv.at[9])
    wg_fin[member] = jnp.sum(wg_mid[...], axis=0) * inv_res
    spread_group(wg_fin.at[member], 10)

    wait_bytes(dw_fin.at[0, pl.ds(0, group // 2 - 1)], recv.at[7])
    remote(dw_fin.at[core], dw_fin.at[core], 14, sibling).start()

    def put_dw(half):
        for chip in range(group // 2):
            for k in range(share):
                at = pl.ds((2 * chip + half) * share + k, width, stride=width)
                ow_buf[at, :] = dw_fin[half, chip, k].astype(F32)

    for half in range(2):
        pl.when(core == half)(functools.partial(put_dw, half))
    wait_bytes(dw_fin.at[0], recv.at[14])
    for half in range(2):
        pl.when(core != half)(functools.partial(put_dw, half))
    ow_copy = pltpu.make_async_copy(ow_buf, ow_hbm, out_sem.at[3])
    ow_copy.start()

    wait_bytes(a_all.at[pl.ds(0, cols - 1)], send.at[0])

    wait_bytes(b_relay, send.at[1])
    for phase, own in zip((2, 13), b_own):

        @pl.when(own)
        def _():
            wait_bytes(db_in.at[pl.ds(0, rows // 2 - 2)], send.at[phase])

        @pl.when(jnp.logical_not(own))
        def _():
            wait_bytes(db_in.at[pl.ds(0, rows // 2)], send.at[phase])

    own_count = jnp.where(
        x == y, b_own[0].astype(jnp.int32) + b_own[1].astype(jnp.int32), 0
    )
    for k in range(3):

        @pl.when(own_count == k)
        def _():
            wait_bytes(db_in.at[pl.ds(0, rows - k)], send.at[3])

    wait_bytes(ln_relay, send.at[15])
    wait_bytes(db_fin, send.at[16])
    wait_bytes(da_in.at[pl.ds(0, cols - 1)], send.at[4])
    wait_bytes(dw_in.at[pl.ds(0, group - 1)], send.at[5])
    wait_bytes(dw_mid.at[pl.ds(0, nz - 1)], send.at[6])
    wait_bytes(dw_fin.at[0, pl.ds(0, group // 2 - 1)], send.at[7])
    wait_bytes(dw_fin.at[0], send.at[14])
    wait_bytes(wg_in.at[pl.ds(0, group - 1)], send.at[8])
    wait_bytes(wg_mid.at[pl.ds(0, nz - 1)], send.at[9])
    wait_bytes(ln_all.at[pl.ds(0, near - 1)], send.at[11])
    wait_bytes(ln_all.at[pl.ds(0, near)], send.at[12])
    wait_bytes(pair_buf, out_sem.at[1])
    align_copy.wait()
    ow_copy.wait()

    wait_bytes(wg_fin.at[pl.ds(0, group - 1)], recv.at[10])
    for h in range(halves):
        for k in range(2 * width // part):
            pw_buf[k * part : (k + 1) * part, h * LANES : (h + 1) * LANES] = wg_fin[
                h * 2 * width // part + k
            ]
    pw_copy = pltpu.make_async_copy(pw_buf, pw_hbm, out_sem.at[4])
    pw_copy.start()

    wait_bytes(wg_fin.at[pl.ds(0, group - 1)], send.at[10])
    pw_copy.wait()

def copy_kernel(*refs):
    sem = refs[8]
    copies = [pltpu.make_async_copy(refs[k], refs[4 + k], sem.at[k]) for k in range(4)]
    for copy in copies:
        copy.start()
    for copy in copies:
        copy.wait()


def on_device(x, gain, shift, we, eshift, wf, fshift, g):
    rows = lax.axis_size("row")
    cols = lax.axis_size("col")
    sl, block, feat = x.shape
    width = we.shape[1] // 2
    ch = wf.shape[1]
    j_len = g.shape[1]
    seqs = sl * cols
    near = cols // 2
    nz = rows // near
    group = near * cols
    share = width // group
    part = feat * 2 * width // LANES // group
    hbm = pl.BlockSpec(memory_space=pl.ANY)

    def buf(*shape, dtype=BF16):
        return pltpu.VMEM(shape, dtype)

    shapes = [
        jax.ShapeDtypeStruct((block, j_len, ch), BF16),
        jax.ShapeDtypeStruct((sl, block, feat), F32),
        jax.ShapeDtypeStruct((width * width, ch), F32),
        jax.ShapeDtypeStruct((2 * width, feat), F32),
    ]
    outs = pl.pallas_call(
        functools.partial(kernel, rows, cols),
        out_shape=shapes,
        in_specs=[hbm] * 8,
        out_specs=[hbm] * 4,
        scratch_shapes=[
            buf(sl, block, feat),
            buf(2 * width, feat),
            buf(1, feat, dtype=F32),
            buf(1, feat, dtype=F32),
            buf(1, 2 * width, dtype=F32),
            buf(1, ch, dtype=F32),
            buf(width * width, ch),
            buf(cols, block, LANES),
            buf(cols, sl * block, feat),
            buf(2, sl * block, feat),
            buf(cols, j_len, LANES),
            buf(block, LANES),
            buf(4, block, LANES),
            buf(j_len, block * ch),
            buf(width * width, ch, dtype=F32),
            buf(LANES, width * ch),
            buf(block * seqs, LANES),
            buf(seqs * width, j_len, dtype=F32),
            buf(seqs * width, j_len),
            buf(block * seqs, cols * block),
            buf(cols * block, block * seqs),
            buf(width * seqs, block * ch),
            buf(block * seqs, width * ch),
            buf(block, j_len, ch),
            buf(sl, block, feat, dtype=F32),
            buf(width * width, ch, dtype=F32),
            buf(2 * width, feat, dtype=F32),
            buf(cols, block, LANES),
            buf(cols, block, LANES),
            buf(cols, j_len, LANES),
            buf(rows, block, LANES),
            buf(2, block, LANES),
            buf(2, block, LANES),
            buf(width, width, ch),
            buf(group, share, width, ch),
            buf(nz, share, width, ch),
            buf(2, group // 2, share, width, ch),
            buf(group, part, LANES, dtype=F32),
            buf(group, part, LANES, dtype=F32),
            buf(nz, part, LANES, dtype=F32),
            buf(group, part, LANES, dtype=F32),
            pltpu.SemaphoreType.REGULAR,
            pltpu.SemaphoreType.DMA((7,)),
            pltpu.SemaphoreType.DMA((5,)),
            pltpu.SemaphoreType.DMA((17,)),
            pltpu.SemaphoreType.DMA((17,)),
        ],
        compiler_params=pltpu.CompilerParams(
            collective_id=0, has_side_effects=True, vmem_limit_bytes=34 * 1024 * 1024
        ),
        cost_estimate=pl.CostEstimate(
            flops=5_000_000_000, bytes_accessed=4_000_000, transcendentals=0
        ),
    )(
        *(
            pltpu.with_memory_space_constraint(v, pltpu.HBM)
            for v in (
                x,
                we.T,
                gain.reshape(1, feat),
                shift.reshape(1, feat),
                eshift.reshape(1, 2 * width),
                fshift.reshape(1, ch),
                wf,
                g,
            )
        )
    )
    pair, align, ow, pw = pl.pallas_call(
        copy_kernel,
        out_shape=shapes,
        in_specs=[hbm] * 4,
        out_specs=[hbm] * 4,
        scratch_shapes=[pltpu.SemaphoreType.DMA((4,))],
        compiler_params=pltpu.CompilerParams(vmem_limit_bytes=16 * 1024 * 1024),
    )(*outs)
    return pair, align, ow, pw.T


def solution(mesh):
    in_specs = (P("col", "row", None), P(), P(), P(), P(), P(), P(), P("row", "col", None))
    out_specs = (P("row", "col", None), P("col", "row", None), P(), P())
    return jax.shard_map(
        on_device, mesh=mesh, in_specs=in_specs, out_specs=out_specs, check_vma=False
    )
```
